512 devices in a mesh: seq: 32 (over x, y, core), expert: 16 (over z).
Axes of the slice: x: 4, y: 4, z: 16, core: 2. Of those that a mesh axis runs over, the one named last changes fastest.
Arguments:
- tokens: bfloat16 [1, 32768, 2048], P(None, 'seq', 'expert'), may hold values from -6 to 6
- slot_params: bfloat16 [256, 2048], P('expert'), may hold values from -16 to 16
- w_in: bfloat16 [16, 2048, 4096], P('expert', None, 'seq'), may hold values from -0.125 to 0.125
- w_out: bfloat16 [16, 4096, 2048], P('expert', 'seq'), may hold values from -0.09375 to 0.09375
- out_grad: bfloat16 [1, 32768, 2048], P(None, 'seq', 'expert'), may hold values from -6 to 6
Outputs:
- mixed: bfloat16 [1, 32768, 2048], P(None, 'seq', 'expert')
- token_grad: bfloat16 [1, 32768, 2048], P(None, 'seq', 'expert')
- param_grad: bfloat16 [256, 2048], P('expert')
- w_in_grad: bfloat16 [16, 2048, 4096], P('expert', None, 'seq')
- w_out_grad: bfloat16 [16, 4096, 2048], P('expert', 'seq')
The draws below stay inside these ranges and needn't reach their ends.
All inputs are finite; a program needn't handle non-finite values.
Results may differ from the reference program's by a relative error of at most 0.033.
Values may be sent and summed in bfloat16 or wider, within the bound.
No kernel may reach another device: no remote copies, remote signals or barrier semaphores. Data moves between devices by JAX's collectives and lax.ppermute only.
A program may use at most 64 MiB of HBM per device.

```python
import math
import jax
import jax.numpy as jnp
from jax import lax

CLIPS = 1
D = 2048
FFW = 4096
S = 16
EXPERTS = 16
N_SLOTS = 256
LEN = 32768


def draw_slot_params(key, part):
    key = jax.random.fold_in(key, 11)
    base_key, scale_key, pick_key, sign_key = jax.random.split(key, 4)
    base = jax.random.truncated_normal(base_key, -3.0, 3.0, (N_SLOTS, D), jnp.float32) / math.sqrt(D)
    scale = jnp.exp(jax.random.uniform(scale_key, (N_SLOTS, 1), jnp.float32, 0.0, math.log(4.0)))
    drawn = jnp.clip(base * scale, -4.0, 4.0)
    chosen = jax.random.permutation(pick_key, N_SLOTS)[:3]
    rows = jnp.arange(N_SLOTS)[:, None]
    strength = jnp.zeros((N_SLOTS, 1), jnp.float32)
    strength = strength + jnp.where(rows == chosen[0], 40.0, 0.0)
    strength = strength + jnp.where(rows == chosen[1], 80.0, 0.0)
    strength = strength + jnp.where(rows == chosen[2], 120.0, 0.0)
    signs = 2.0 * jax.random.bernoulli(sign_key, 0.5, (N_SLOTS, D)).astype(jnp.float32) - 1.0
    strong = signs * strength / math.sqrt(D)
    return jnp.where(strength > 0.0, strong, drawn).astype(jnp.bfloat16)


def levels(own_key, extent, cuts, least, high):
    factor_of, own = 1.0, jax.random.fold_in(own_key, 6)
    for axis_at, parts in cuts:
        heights = jnp.exp(jax.random.uniform(jax.random.fold_in(own, axis_at), (parts,), jnp.float32, least / len(cuts), high / len(cuts)))
        factor_of = factor_of * jnp.repeat(heights, extent[axis_at] // parts).reshape([-1 if axis == axis_at else 1 for axis in range(len(extent))])
    return factor_of


def gaussian(key, dims, deviation, limit, pieces=(), kind=jnp.bfloat16):
    level = levels(key, dims, pieces, -0.22, 0.18) if pieces else 1.0
    array = jax.random.normal(key, dims, jnp.float32) * deviation * level
    return jnp.minimum(jnp.maximum(array, -limit), limit).astype(kind)


def setup_inputs(seed: int = 0) -> dict:
    splits = jax.random.split(jax.random.key(seed), 6)
    tokens = gaussian(splits[0], (CLIPS, LEN, D), 1.0, 6.0, ((1, 32), (2, 16)))
    slot_params = draw_slot_params(jax.random.fold_in(splits[5], 71), 0)
    w_in = gaussian(splits[2], (EXPERTS, D, FFW), D ** -0.5, 0.125, ((0, 16), (2, 32)))
    w_out = gaussian(splits[3], (EXPERTS, FFW, D), FFW ** -0.5, 0.09375, ((0, 16), (1, 32)))
    out_grad = gaussian(splits[4], (CLIPS, LEN, D), 1.0, 6.0, ((1, 32), (2, 16)))
    return dict(tokens=tokens, slot_params=slot_params, w_in=w_in, w_out=w_out, out_grad=out_grad)


def gelu_exact(values):
    return jax.nn.gelu(values, approximate=False)

def reference(tokens, slot_params, w_in, w_out, out_grad):
    bfloat = jnp.bfloat16
    single = jnp.float32
    dispatch_list = []
    dispatch_low_list = []
    combine_list = []
    combine_low_list = []
    slot_low_list = []
    for clip_index in range(CLIPS):
        clip_tokens = tokens[clip_index]
        logits = jnp.dot(slot_params, clip_tokens.T, preferred_element_type=single)
        raised = jnp.exp(logits - lax.optimization_barrier(jnp.max(logits, axis=1, keepdims=True)))
        dispatch = raised / lax.optimization_barrier(jnp.sum(raised, axis=1, keepdims=True))
        dispatch_low = dispatch.astype(bfloat)
        slot_low_list.append(jnp.dot(dispatch_low, clip_tokens, preferred_element_type=single).astype(bfloat))
        lifted = jnp.exp(logits - lax.optimization_barrier(jnp.max(logits, axis=0, keepdims=True)))
        combine = lifted / lax.optimization_barrier(jnp.sum(lifted, axis=0, keepdims=True))
        dispatch_list.append(dispatch)
        dispatch_low_list.append(dispatch_low)
        combine_list.append(combine)
        combine_low_list.append(combine.astype(bfloat))
    slot_low = jnp.stack(slot_low_list, axis=1)
    slot_rows = slot_low.reshape(EXPERTS, S, CLIPS, D).astype(single)
    weight_in = w_in.astype(single)
    weight_out = w_out.astype(single)
    preact = jnp.einsum('escd,edf->escf', slot_rows, weight_in)
    hidden_low = gelu_exact(preact).astype(bfloat)
    expert_out = jnp.einsum('escf,efd->escd', hidden_low.astype(single), weight_out)
    out_low = expert_out.astype(bfloat).reshape(N_SLOTS, CLIPS, D)
    mixed_list = []
    slot_grad_list = []
    combine_cot_list = []
    for clip_index in range(CLIPS):
        clip_grad = out_grad[clip_index]
        combine_low = combine_low_list[clip_index]
        mixed_list.append(jnp.dot(combine_low.T, out_low[:, clip_index], preferred_element_type=single).astype(bfloat))
        combine_cot_list.append(jnp.dot(out_low[:, clip_index], clip_grad.T, preferred_element_type=single))
        slot_grad_list.append(jnp.dot(combine_low, clip_grad, preferred_element_type=single))
    slot_grad_low = jnp.stack(slot_grad_list, axis=1).astype(bfloat)
    grad_rows = slot_grad_low.reshape(EXPERTS, S, CLIPS, D).astype(single)
    w_out_grad = jnp.einsum('escf,escd->efd', hidden_low.astype(single), grad_rows).astype(bfloat)
    hidden_grad = jnp.einsum('escd,efd->escf', grad_rows, weight_out)
    unused, pullback = jax.vjp(gelu_exact, preact)
    preact_low = pullback(hidden_grad)[0].astype(bfloat)
    w_in_grad = jnp.einsum('escd,escf->edf', slot_rows, preact_low.astype(single)).astype(bfloat)
    input_low = jnp.einsum('escf,edf->escd', preact_low.astype(single), weight_in).astype(bfloat)
    input_low = input_low.reshape(N_SLOTS, CLIPS, D)
    token_grad_list = []
    param_total = jnp.zeros((N_SLOTS, D), single)
    for clip_index in range(CLIPS):
        clip_tokens = tokens[clip_index]
        combine = combine_list[clip_index]
        combine_low = combine_low_list[clip_index]
        dispatch = dispatch_list[clip_index]
        dispatch_low = dispatch_low_list[clip_index]
        combine_cot = combine_cot_list[clip_index]
        row_sum = lax.optimization_barrier(jnp.sum(combine_low.astype(single) * combine_cot, axis=0, keepdims=True))
        dispatch_cot = jnp.dot(input_low[:, clip_index], clip_tokens.T, preferred_element_type=single)
        column_sum = lax.optimization_barrier(jnp.sum(dispatch_low.astype(single) * dispatch_cot, axis=1, keepdims=True))
        logit_low = (dispatch * (dispatch_cot - column_sum) + combine * (combine_cot - row_sum)).astype(bfloat)
        token_part = jnp.dot(dispatch_low.T, input_low[:, clip_index], preferred_element_type=single)
        token_part = token_part + jnp.dot(logit_low.T, slot_params, preferred_element_type=single)
        token_grad_list.append(token_part.astype(bfloat))
        param_total = param_total + jnp.dot(logit_low, clip_tokens, preferred_element_type=single)
    mixed = jnp.stack(mixed_list, axis=0)
    token_grad = jnp.stack(token_grad_list, axis=0)
    return (mixed, token_grad, param_total.astype(bfloat), w_in_grad, w_out_grad)
```

```python
import functools

import jax
import jax.numpy as jnp
from jax import lax
from jax.experimental import pallas as pl
from jax.experimental.pallas import tpu as pltpu
from jax.sharding import PartitionSpec as P

BF = jnp.bfloat16
F32 = jnp.float32
INTERPRET = False


def call(body, out_shape, *args):
    vmem, smem = (pl.BlockSpec(memory_space=kind) for kind in (pltpu.VMEM, pltpu.SMEM))
    return pl.pallas_call(
        body,
        out_shape=out_shape,
        in_specs=[smem if arg.dtype == jnp.int32 else vmem for arg in args],
        interpret=INTERPRET,
        compiler_params=pltpu.CompilerParams(vmem_limit_bytes=48 * 1024 * 1024),
    )(*args)


def shape(dims, kind):
    return jax.ShapeDtypeStruct(dims, kind)


def nt(a, b):
    return lax.dot_general(a, b, (((1,), (1,)), ((), ())), preferred_element_type=F32)


def tn(a, b):
    return lax.dot_general(a, b, (((0,), (0,)), ((), ())), preferred_element_type=F32)


def nn(a, b):
    return jnp.dot(a, b, preferred_element_type=F32)


def split3(value):
    high = value.astype(BF).astype(F32)
    rest = value - high
    mid = rest.astype(BF).astype(F32)
    return [high, mid, (rest - mid).astype(BF).astype(F32)]


def lanes(ref, rows=slice(None)):
    return jnp.concatenate([ref[f, rows, :] for f in range(16)], axis=1)


def tokens_of(z_ref):
    count = (z_ref.shape[1] - 8) // 2
    return lanes(z_ref, slice(0, count)), lanes(z_ref, slice(count, 2 * count))


def route_kernel(pown_ref, pother_ref, z_ref, own_ref, other_ref, logit_ref, comb_ref):
    x, g = tokens_of(z_ref)
    logits = jnp.concatenate([nt(x, lanes(ref)) for ref in (pown_ref, pother_ref)], axis=1)
    logit_ref[...] = logits
    peak = jnp.max(logits, axis=0, keepdims=True)
    raised = jnp.exp(logits - peak)
    total = jnp.sum(raised, axis=0, keepdims=True)
    lifted = jnp.exp(logits - jnp.max(logits, axis=1, keepdims=True))
    combine = lifted / jnp.sum(lifted, axis=1, keepdims=True)
    comb_ref[...] = combine
    stats = jnp.concatenate(
        split3(peak) + split3(total) + [jnp.zeros((10, 256), F32)], axis=0
    ).astype(BF)
    for pay_ref, cols in ((own_ref, slice(0, 128)), (other_ref, slice(128, 256))):
        part_in = tn(raised[:, cols].astype(BF), x).astype(BF)
        part_grad = tn(combine[:, cols].astype(BF), g).astype(BF)
        for f in range(16):
            feats = slice(f * 128, (f + 1) * 128)
            pay_ref[f, 0:128, :] = part_in[:, feats]
            pay_ref[f, 128:256, :] = part_grad[:, feats]
            pay_ref[f, 256:272, :] = stats[:, cols]


def rescale(stats):
    peaks = jnp.concatenate([s[0:1] + s[1:2] + s[2:3] for s in stats], axis=0)
    totals = jnp.concatenate([s[3:4] + s[4:5] + s[5:6] for s in stats], axis=0)
    peak = jnp.max(peaks, axis=0, keepdims=True)
    scale = jnp.exp(peaks - peak)
    total = jnp.sum(scale * totals, axis=0, keepdims=True)
    rows = split3(peak) + split3(total)
    pad = jnp.zeros((122 - len(stats), 128), F32)
    return rows, jnp.concatenate([scale] + rows + [pad], axis=0).T


def merge_core_kernel(own_ref, sib_ref, pay_ref):
    rows, columns = rescale([ref[0, 256:272, :].astype(F32) for ref in (own_ref, sib_ref)])
    stats = jnp.concatenate(rows + [jnp.zeros((10, 128), F32)], axis=0).astype(BF)
    for f in range(16):
        pay_ref[f, 0:128, :] = (
            columns[:, 0:1] * own_ref[f, 0:128, :].astype(F32)
            + columns[:, 1:2] * sib_ref[f, 0:128, :].astype(F32)
        ).astype(BF)
        pay_ref[f, 128:256, :] = (
            own_ref[f, 128:256, :].astype(F32) + sib_ref[f, 128:256, :].astype(F32)
        ).astype(BF)
        pay_ref[f, 256:272, :] = stats


def merge_seq_kernel(r_ref, pay_ref):
    rows, columns = rescale([r_ref[i, 256:272, :].astype(F32) for i in range(16)])
    sum_in = jnp.zeros((128, 128), F32)
    sum_grad = jnp.zeros((128, 128), F32)
    for i in range(16):
        sum_in = sum_in + columns[:, i : i + 1] * r_ref[i, 0:128, :].astype(F32)
        sum_grad = sum_grad + r_ref[i, 128:256, :].astype(F32)
    for e in range(16):
        rows = slice(e * 8, (e + 1) * 8)
        pay_ref[e] = jnp.concatenate(
            [sum_in[rows], sum_grad[rows], columns[rows]], axis=0
        ).astype(BF)


def merge_expert_kernel(r_ref, pay_ref, slot_ref, log_ref):
    blocks = [r_ref[i].astype(F32) for i in range(16)]
    peaks = [b[16:24, 16:17] + b[16:24, 17:18] + b[16:24, 18:19] for b in blocks]
    totals = [b[16:24, 19:20] + b[16:24, 20:21] + b[16:24, 21:22] for b in blocks]
    peak = functools.reduce(jnp.maximum, peaks)
    slot = jnp.zeros((8, 128), F32)
    grad = jnp.zeros((8, 128), F32)
    total = jnp.zeros((8, 1), F32)
    for i in range(16):
        scale = jnp.exp(peaks[i] - peak)
        slot = slot + scale * blocks[i][0:8]
        total = total + scale * totals[i]
        grad = grad + blocks[i][8:16]
    slot = slot / total
    slot_ref[...] = slot
    log_ref[...] = jnp.broadcast_to(peak + jnp.log(total), (8, 128))
    both = jnp.concatenate([slot, grad], axis=0).astype(BF)
    for i in range(32):
        pay_ref[i] = both


def expert_kernel(r_ref, win_ref, wout_ref, pay_ref, slot_ref, grad_ref, hidden_ref, pre_ref):
    blocks = [r_ref[i].astype(F32) for i in range(32)]

    def rows(first):
        return jnp.concatenate(
            [
                jnp.concatenate(
                    [blocks[2 * f][first : first + 8], blocks[2 * f + 1][first : first + 8]],
                    axis=0,
                )
                for f in range(16)
            ],
            axis=1,
        ).astype(BF)

    slot, grad = rows(0), rows(8)
    preact = nn(slot, win_ref[...])
    cdf = 0.5 * (1.0 + lax.erf(preact * 0.7071067811865476))
    density = 0.3989422804014327 * jnp.exp(-0.5 * preact * preact)
    hidden = (preact * cdf).astype(BF)
    hidden_grad = nt(grad, wout_ref[...])
    pre = (hidden_grad * (cdf + preact * density)).astype(BF)
    out_part = nn(hidden, wout_ref[...])
    in_part = nt(pre, win_ref[...])
    for h in range(2):
        for f in range(16):
            rows_, feats = slice(h * 8, h * 8 + 8), slice(f * 128, (f + 1) * 128)
            pay_ref[f * 2 + h] = jnp.concatenate(
                [out_part[rows_, feats], in_part[rows_, feats]], axis=0
            ).astype(BF)
    slot_ref[...] = slot
    grad_ref[...] = grad
    hidden_ref[...] = hidden
    pre_ref[...] = pre


def out_merge_kernel(r_ref, slot_ref, log_ref, pay_ref):
    both = functools.reduce(jnp.add, [r_ref[i].astype(F32) for i in range(32)])
    both = both.astype(BF).astype(F32)
    guess = jnp.sum(both[8:16] * slot_ref[...], axis=1, keepdims=True)
    lane = lax.broadcasted_iota(jnp.int32, (8, 128), 1)
    stats = jnp.zeros((8, 128), F32)
    for at, value in enumerate(split3(log_ref[...][:, 0:1]) + split3(guess)):
        stats = jnp.where(lane == at, value, stats)
    both = jnp.concatenate([both, stats], axis=0).astype(BF)
    for i in range(16):
        pay_ref[i] = both


def spread_kernel(r_ref, pay_ref):
    blocks = [r_ref[i].astype(F32) for i in range(16)]
    out = jnp.concatenate([b[0:8] for b in blocks], axis=0).astype(BF)
    inp = jnp.concatenate([b[8:16] for b in blocks], axis=0).astype(BF)
    stats = jnp.concatenate([b[16:24] for b in blocks], axis=0).T[0:16].astype(BF)
    for i in range(16):
        pay_ref[i, 0:128, :] = out
        pay_ref[i, 128:256, :] = inp
        pay_ref[i, 256:272, :] = stats


def mix_kernel(
    own_ref, other_ref, z_ref, logit_ref, comb_ref,
    mixed_ref, parown_ref, parother_ref, guess_ref, disp_ref, cot_ref, term_ref, in_ref,
):
    x, g = tokens_of(z_ref)
    combine = comb_ref[...]
    combine_low = combine.astype(BF)
    pair = (own_ref, other_ref)
    stats = [ref[0, 256:272, :].astype(F32) for ref in pair]
    logs = jnp.concatenate([s[0:1] + s[1:2] + s[2:3] for s in stats], axis=1)
    sums = [
        functools.reduce(jnp.add, [ref[f, 256:272, :].astype(F32) for f in range(16)])
        for ref in pair
    ]
    guess = jnp.concatenate([s[3:4] + s[4:5] + s[5:6] for s in sums], axis=1)
    outs = jnp.concatenate([lanes(ref, slice(0, 128)) for ref in pair], axis=0)
    ins = jnp.concatenate([lanes(ref, slice(128, 256)) for ref in pair], axis=0)
    dispatch_cot = nt(x, ins)
    dispatch = jnp.exp(logit_ref[...] - logs)
    column = jnp.sum(dispatch.astype(BF).astype(F32) * dispatch_cot, axis=0, keepdims=True)
    combine_cot = nt(g, outs)
    row_sum = jnp.sum(combine_low.astype(F32) * combine_cot, axis=1, keepdims=True)
    term = combine * (combine_cot - row_sum)
    logit_low = (dispatch * (dispatch_cot - guess) + term).astype(BF)
    for ref, half in ((parown_ref, slice(0, 128)), (parother_ref, slice(128, 256))):
        part = tn(logit_low[:, half], x).astype(BF)
        sums = jnp.concatenate(
            split3(column[:, half]) + [jnp.zeros((13, 128), F32)], axis=0
        ).astype(BF)
        for f in range(16):
            ref[f, 0:128, :] = part[:, f * 128 : (f + 1) * 128]
            ref[f, 128:144, :] = sums
    mixed = nn(combine_low, outs).astype(BF)
    for f in range(16):
        mixed_ref[f] = mixed[:, f * 128 : (f + 1) * 128]
    guess_ref[...] = jnp.broadcast_to(guess, (8, 256))
    disp_ref[...] = dispatch
    cot_ref[...] = dispatch_cot
    term_ref[...] = term
    in_ref[...] = ins


def column_of(block):
    return block[0:1] + block[1:2] + block[2:3]


def param_core_kernel(own_ref, sib_ref, pay_ref):
    sums = [ref[0, 128:144, :].astype(F32) for ref in (own_ref, sib_ref)]
    sums = jnp.concatenate(
        split3(column_of(sums[0]) + column_of(sums[1])) + [jnp.zeros((13, 128), F32)], axis=0
    ).astype(BF)
    for f in range(16):
        pay_ref[f, 0:128, :] = (
            own_ref[f, 0:128, :].astype(F32) + sib_ref[f, 0:128, :].astype(F32)
        ).astype(BF)
        pay_ref[f, 128:144, :] = sums


def param_seq_kernel(r_ref, mixed_ref, pay_ref):
    count = mixed_ref.shape[1]
    total = functools.reduce(jnp.add, [r_ref[i, 0:128, :].astype(F32) for i in range(16)])
    column = functools.reduce(
        jnp.add, [column_of(r_ref[i, 128:144, :].astype(F32)) for i in range(16)]
    )
    sums = jnp.concatenate(split3(column) + [jnp.zeros((5, 128), F32)], axis=0)
    for e in range(16):
        pay_ref[e, 0:count, :] = mixed_ref[e]
        pay_ref[e, count : count + 16, :] = jnp.concatenate(
            [total[e * 8 : (e + 1) * 8], sums], axis=0
        ).astype(BF)


def param_expert_kernel(at_ref, r_ref, guess_ref, slot_ref, pay_ref, col_ref):
    count = r_ref.shape[1] - 16
    total = functools.reduce(
        jnp.add, [r_ref[i, count : count + 16, :].astype(F32) for i in range(16)]
    )
    column = column_of(total[8:16])
    col_ref[...] = jnp.broadcast_to(column, (8, 128))
    missed = column - guess_ref[0:1, 0:128]
    lane = lax.broadcasted_iota(jnp.int32, (8, 128), 1)
    row = lax.broadcasted_iota(jnp.int32, (8, 128), 0)
    missed = jnp.sum(
        jnp.where(lane == at_ref[0] * 8 + row, missed, 0.0), axis=1, keepdims=True
    )
    param = total[0:8] - missed * slot_ref[...]
    for i in range(32):
        pay_ref[i] = param


def token_kernel(
    colown_ref, colother_ref, pown_ref, pother_ref, disp_ref, cot_ref, term_ref, in_ref, tok_ref
):
    column = jnp.concatenate([colown_ref[0:1, :], colother_ref[0:1, :]], axis=1)
    params = jnp.concatenate([lanes(pown_ref), lanes(pother_ref)], axis=0)
    dispatch = disp_ref[...]
    logit_low = (dispatch * (cot_ref[...] - column) + term_ref[...]).astype(BF)
    token_grad = (nn(dispatch.astype(BF), in_ref[...]) + nn(logit_low, params)).astype(BF)
    for f in range(16):
        tok_ref[f] = token_grad[:, f * 128 : (f + 1) * 128]


CHIPS = [list(range(0, 32, 2)), list(range(1, 32, 2))]
SIBLING = [(i, i ^ 1) for i in range(32)]


def swap(array, axis, groups=None):
    return lax.all_to_all(
        array, axis, split_axis=0, concat_axis=0, tiled=True, axis_index_groups=groups
    )


def local(tokens, slot_params, w_in, w_out, out_grad):
    count = tokens.shape[1] // 16
    seq_at = lax.axis_index("seq")
    expert_at = lax.axis_index("expert").astype(jnp.int32).reshape(1)
    piece = lax.dynamic_slice(
        slot_params, ((seq_at % 2) * 8, (seq_at // 2) * 128), (8, 128)
    )
    block = jnp.concatenate(
        [
            tokens.reshape(16, count, 128),
            out_grad.reshape(16, count, 128),
            jnp.broadcast_to(piece[None], (16, 8, 128)),
        ],
        axis=1,
    )
    z = swap(block, "expert")
    mine = z[:, 2 * count :].reshape(128, 128)
    params = swap(jnp.broadcast_to(mine[None], (16, 128, 128)), "seq", CHIPS)
    params_other = lax.ppermute(params, "seq", SIBLING)

    half = shape((16, 272, 128), BF)
    slots = shape((count, 256), F32)
    small = shape((16, 24, 128), BF)
    row = shape((8, 128), F32)
    own, other, logits, combine = call(
        route_kernel, (half, half, slots, slots), params, params_other, z
    )
    sibling = lax.ppermute(other, "seq", SIBLING)
    pay = call(merge_core_kernel, half, own, sibling)
    pay = call(merge_seq_kernel, small, swap(pay, "seq", CHIPS))
    pay, slot_piece, log_piece = call(
        merge_expert_kernel, (shape((32, 16, 128), BF), row, row), swap(pay, "expert")
    )
    pay, slot_low, grad_low, hidden, pre = call(
        expert_kernel,
        (
            shape((32, 16, 128), BF),
            shape((16, 2048), BF),
            shape((16, 2048), BF),
            shape((16, 128), BF),
            shape((16, 128), BF),
        ),
        swap(pay, "seq"),
        w_in[0],
        w_out[0],
    )
    w_out_grad = tn(hidden, grad_low).astype(BF)
    w_in_grad = tn(slot_low, pre).astype(BF)
    pay = call(out_merge_kernel, small, swap(pay, "seq"), slot_piece, log_piece)
    pay = call(spread_kernel, half, swap(pay, "expert"))
    own = swap(pay, "seq", CHIPS)
    other = lax.ppermute(own, "seq", SIBLING)
    part = shape((16, 144, 128), BF)
    by_feature = shape((16, count, 128), BF)
    mixed, own, other, guess, dispatch, dispatch_cot, term, ins = call(
        mix_kernel,
        (
            by_feature, part, part, shape((8, 256), F32),
            slots, slots, slots, shape((256, 2048), BF),
        ),
        own,
        other,
        z,
        logits,
        combine,
    )
    pay = call(param_core_kernel, part, own, lax.ppermute(other, "seq", SIBLING))
    pay = call(
        param_seq_kernel, shape((16, count + 16, 128), BF), swap(pay, "seq", CHIPS), mixed
    )
    pay = swap(pay, "expert")
    mixed = pay[:, 0:count].reshape(tokens.shape)
    param_grad, column = call(
        param_expert_kernel, (shape((32, 8, 128), F32), row), expert_at, pay, guess, slot_piece
    )
    token_grad = call(
        token_kernel,
        by_feature,
        column,
        lax.ppermute(column, "seq", SIBLING),
        params,
        params_other,
        dispatch,
        dispatch_cot,
        term,
        ins,
    )
    token_grad = swap(token_grad, "expert").reshape(tokens.shape)
    param_grad = swap(param_grad, "seq")
    param_grad = (
        param_grad.reshape(16, 2, 8, 128).transpose(1, 2, 0, 3).reshape(16, 2048).astype(BF)
    )
    return (mixed, token_grad, param_grad, w_in_grad[None], w_out_grad[None])


def solution(mesh):
    return jax.shard_map(
        local,
        mesh=mesh,
        in_specs=(
            P(None, "seq", "expert"),
            P("expert", None),
            P("expert", None, "seq"),
            P("expert", "seq", None),
            P(None, "seq", "expert"),
        ),
        out_specs=(
            P(None, "seq", "expert"),
            P(None, "seq", "expert"),
            P("expert", None),
            P("expert", None, "seq"),
            P("expert", "seq", None),
        ),
        check_vma=False,
    )
```

```python
import functools

import jax
import jax.numpy as jnp
from jax import lax
from jax.experimental import pallas as pl
from jax.experimental.pallas import tpu as pltpu
from jax.sharding import PartitionSpec as P

BF = jnp.bfloat16
F32 = jnp.float32
INTERPRET = False


def call(body, out_shape, *args):
    vmem, smem = (pl.BlockSpec(memory_space=kind) for kind in (pltpu.VMEM, pltpu.SMEM))
    return pl.pallas_call(
        body,
        out_shape=out_shape,
        in_specs=[smem if arg.dtype == jnp.int32 else vmem for arg in args],
        interpret=INTERPRET,
        compiler_params=pltpu.CompilerParams(vmem_limit_bytes=48 * 1024 * 1024),
    )(*args)


def shape(dims, kind):
    return jax.ShapeDtypeStruct(dims, kind)


def nt(a, b):
    return lax.dot_general(a, b, (((1,), (1,)), ((), ())), preferred_element_type=F32)


def tn(a, b):
    return lax.dot_general(a, b, (((0,), (0,)), ((), ())), preferred_element_type=F32)


def nn(a, b):
    return jnp.dot(a, b, preferred_element_type=F32)


def split3(value):
    high = value.astype(BF).astype(F32)
    rest = value - high
    mid = rest.astype(BF).astype(F32)
    return [high, mid, (rest - mid).astype(BF).astype(F32)]


def lanes(ref, rows=slice(None)):
    return jnp.concatenate([ref[f, rows, :] for f in range(16)], axis=1)


def chip_order(at_ref):
    masks = [at_ref[1] ^ f for f in range(16)]
    return [m ^ ((m >> 1) & 5) for m in masks]


def stage_kernel(z_ref, g_ref, mine_ref, out_ref):
    count = g_ref.shape[1]
    blocks = [z_ref[f].astype(F32)[count:] for f in range(16)]
    mine_ref[0] = jnp.concatenate(blocks, axis=0).astype(BF)
    out_ref[...] = g_ref[...]


def route_kernel(
    at_ref, pown_ref, pother_ref, z_ref, g_ref, own_ref, other_ref, logit_ref, comb_ref, par_ref
):
    x = lanes(z_ref, slice(0, g_ref.shape[1]))
    g = lanes(g_ref)
    order = chip_order(at_ref)
    params = jnp.concatenate(
        [
            jnp.concatenate([ref[j] for j in order], axis=1)
            for ref in (pown_ref, pother_ref)
        ],
        axis=0,
    )
    par_ref[...] = params
    logits = nt(x, params)
    logit_ref[...] = logits
    peak = jnp.max(logits, axis=0, keepdims=True)
    raised = jnp.exp(logits - peak)
    total = jnp.sum(raised, axis=0, keepdims=True)
    lifted = jnp.exp(logits - jnp.max(logits, axis=1, keepdims=True))
    combine = lifted / jnp.sum(lifted, axis=1, keepdims=True)
    comb_ref[...] = combine
    stats = jnp.concatenate(
        split3(peak) + split3(total) + [jnp.zeros((10, 256), F32)], axis=0
    ).astype(BF)
    for pay_ref, cols in ((own_ref, slice(0, 128)), (other_ref, slice(128, 256))):
        part_in = tn(raised[:, cols].astype(BF), x).astype(BF)
        part_grad = tn(combine[:, cols].astype(BF), g).astype(BF)
        for f in range(16):
            feats = slice(f * 128, (f + 1) * 128)
            pay_ref[f, 0:128, :] = part_in[:, feats]
            pay_ref[f, 128:256, :] = part_grad[:, feats]
            pay_ref[f, 256:272, :] = stats[:, cols]


def rescale(stats):
    peaks = jnp.concatenate([s[0:1] + s[1:2] + s[2:3] for s in stats], axis=0)
    totals = jnp.concatenate([s[3:4] + s[4:5] + s[5:6] for s in stats], axis=0)
    peak = jnp.max(peaks, axis=0, keepdims=True)
    scale = jnp.exp(peaks - peak)
    total = jnp.sum(scale * totals, axis=0, keepdims=True)
    rows = split3(peak) + split3(total)
    pad = jnp.zeros((122 - len(stats), 128), F32)
    return rows, jnp.concatenate([scale] + rows + [pad], axis=0).T


def merge_core_kernel(own_ref, sib_ref, pay_ref):
    rows, columns = rescale([ref[0, 256:272, :].astype(F32) for ref in (own_ref, sib_ref)])
    stats = jnp.concatenate(rows + [jnp.zeros((10, 128), F32)], axis=0).astype(BF)
    for f in range(16):
        pay_ref[f, 0:128, :] = (
            columns[:, 0:1] * own_ref[f, 0:128, :].astype(F32)
            + columns[:, 1:2] * sib_ref[f, 0:128, :].astype(F32)
        ).astype(BF)
        pay_ref[f, 128:256, :] = (
            own_ref[f, 128:256, :].astype(F32) + sib_ref[f, 128:256, :].astype(F32)
        ).astype(BF)
        pay_ref[f, 256:272, :] = stats


def merge_seq_kernel(r_ref, pay_ref):
    rows, columns = rescale([r_ref[i, 256:272, :].astype(F32) for i in range(16)])
    sum_in = jnp.zeros((128, 128), F32)
    sum_grad = jnp.zeros((128, 128), F32)
    for i in range(16):
        sum_in = sum_in + columns[:, i : i + 1] * r_ref[i, 0:128, :].astype(F32)
        sum_grad = sum_grad + r_ref[i, 128:256, :].astype(F32)
    for e in range(16):
        rows = slice(e * 8, (e + 1) * 8)
        pay_ref[e] = jnp.concatenate(
            [sum_in[rows], sum_grad[rows], columns[rows]], axis=0
        ).astype(BF)


def merge_expert_kernel(r_ref, pay_ref, slot_ref, log_ref):
    blocks = [r_ref[i].astype(F32) for i in range(16)]
    peaks = [b[16:24, 16:17] + b[16:24, 17:18] + b[16:24, 18:19] for b in blocks]
    totals = [b[16:24, 19:20] + b[16:24, 20:21] + b[16:24, 21:22] for b in blocks]
    peak = functools.reduce(jnp.maximum, peaks)
    slot = jnp.zeros((8, 128), F32)
    grad = jnp.zeros((8, 128), F32)
    total = jnp.zeros((8, 1), F32)
    for i in range(16):
        scale = jnp.exp(peaks[i] - peak)
        slot = slot + scale * blocks[i][0:8]
        total = total + scale * totals[i]
        grad = grad + blocks[i][8:16]
    slot = slot / total
    slot_ref[...] = slot
    log_ref[...] = jnp.broadcast_to(peak + jnp.log(total), (8, 128))
    both = jnp.concatenate([slot, grad], axis=0).astype(BF)
    for i in range(32):
        pay_ref[i] = both


def expert_kernel(r_ref, win_ref, wout_ref, pay_ref, slot_ref, grad_ref, hidden_ref, pre_ref):
    blocks = [r_ref[i].astype(F32) for i in range(32)]

    def rows(first):
        return jnp.concatenate(
            [
                jnp.concatenate(
                    [blocks[2 * f][first : first + 8], blocks[2 * f + 1][first : first + 8]],
                    axis=0,
                )
                for f in range(16)
            ],
            axis=1,
        ).astype(BF)

    slot, grad = rows(0), rows(8)
    preact = nn(slot, win_ref[...])
    cdf = 0.5 * (1.0 + lax.erf(preact * 0.7071067811865476))
    density = 0.3989422804014327 * jnp.exp(-0.5 * preact * preact)
    hidden = (preact * cdf).astype(BF)
    hidden_grad = nt(grad, wout_ref[...])
    pre = (hidden_grad * (cdf + preact * density)).astype(BF)
    out_part = nn(hidden, wout_ref[...])
    in_part = nt(pre, win_ref[...])
    for h in range(2):
        for f in range(16):
            rows_, feats = slice(h * 8, h * 8 + 8), slice(f * 128, (f + 1) * 128)
            pay_ref[f * 2 + h] = jnp.concatenate(
                [out_part[rows_, feats], in_part[rows_, feats]], axis=0
            ).astype(BF)
    slot_ref[...] = slot
    grad_ref[...] = grad
    hidden_ref[...] = hidden
    pre_ref[...] = pre


def out_merge_kernel(r_ref, slot_ref, log_ref, pay_ref):
    both = functools.reduce(jnp.add, [r_ref[i].astype(F32) for i in range(32)])
    both = both.astype(BF).astype(F32)
    guess = jnp.sum(both[8:16] * slot_ref[...], axis=1, keepdims=True)
    lane = lax.broadcasted_iota(jnp.int32, (8, 128), 1)
    stats = jnp.zeros((8, 128), F32)
    for at, value in enumerate(split3(log_ref[...][:, 0:1]) + split3(guess)):
        stats = jnp.where(lane == at, value, stats)
    both = jnp.concatenate([both, stats], axis=0).astype(BF)
    for i in range(16):
        pay_ref[i] = both


def spread_kernel(r_ref, pay_ref):
    blocks = [r_ref[i].astype(F32) for i in range(16)]
    out = jnp.concatenate([b[0:8] for b in blocks], axis=0).astype(BF)
    inp = jnp.concatenate([b[8:16] for b in blocks], axis=0).astype(BF)
    stats = jnp.concatenate([b[16:24] for b in blocks], axis=0).T[0:16].astype(BF)
    for i in range(16):
        pay_ref[i, 0:128, :] = out
        pay_ref[i, 128:256, :] = inp
        pay_ref[i, 256:272, :] = stats


def mix_kernel(
    own_ref, other_ref, z_ref, g_ref, logit_ref, comb_ref,
    mixed_ref, parown_ref, parother_ref, guess_ref, disp_ref, cot_ref, term_ref, in_ref,
):
    x = lanes(z_ref, slice(0, g_ref.shape[1]))
    g = lanes(g_ref)
    combine = comb_ref[...]
    combine_low = combine.astype(BF)
    pair = (own_ref, other_ref)
    stats = [ref[0, 256:272, :].astype(F32) for ref in pair]
    logs = jnp.concatenate([s[0:1] + s[1:2] + s[2:3] for s in stats], axis=1)
    sums = [
        functools.reduce(jnp.add, [ref[f, 256:272, :].astype(F32) for f in range(16)])
        for ref in pair
    ]
    guess = jnp.concatenate([s[3:4] + s[4:5] + s[5:6] for s in sums], axis=1)
    outs = jnp.concatenate([lanes(ref, slice(0, 128)) for ref in pair], axis=0)
    ins = jnp.concatenate([lanes(ref, slice(128, 256)) for ref in pair], axis=0)
    dispatch_cot = nt(x, ins)
    dispatch = jnp.exp(logit_ref[...] - logs)
    column = jnp.sum(dispatch.astype(BF).astype(F32) * dispatch_cot, axis=0, keepdims=True)
    combine_cot = nt(g, outs)
    row_sum = jnp.sum(combine_low.astype(F32) * combine_cot, axis=1, keepdims=True)
    term = combine * (combine_cot - row_sum)
    logit_low = (dispatch * (dispatch_cot - guess) + term).astype(BF)
    for ref, half in ((parown_ref, slice(0, 128)), (parother_ref, slice(128, 256))):
        part = tn(logit_low[:, half], x).astype(BF)
        sums = jnp.concatenate(
            split3(column[:, half]) + [jnp.zeros((13, 128), F32)], axis=0
        ).astype(BF)
        for f in range(16):
            ref[f, 0:128, :] = part[:, f * 128 : (f + 1) * 128]
            ref[f, 128:144, :] = sums
    mixed = nn(combine_low, outs).astype(BF)
    for f in range(16):
        mixed_ref[f] = mixed[:, f * 128 : (f + 1) * 128]
    guess_ref[...] = jnp.broadcast_to(guess, (8, 256))
    disp_ref[...] = dispatch
    cot_ref[...] = dispatch_cot
    term_ref[...] = term
    in_ref[...] = ins


def column_of(block):
    return block[0:1] + block[1:2] + block[2:3]


def param_core_kernel(own_ref, sib_ref, pay_ref):
    sums = [ref[0, 128:144, :].astype(F32) for ref in (own_ref, sib_ref)]
    sums = jnp.concatenate(
        split3(column_of(sums[0]) + column_of(sums[1])) + [jnp.zeros((13, 128), F32)], axis=0
    ).astype(BF)
    for f in range(16):
        pay_ref[f, 0:128, :] = (
            own_ref[f, 0:128, :].astype(F32) + sib_ref[f, 0:128, :].astype(F32)
        ).astype(BF)
        pay_ref[f, 128:144, :] = sums


def param_seq_kernel(r_ref, mixed_ref, pay_ref):
    count = mixed_ref.shape[1]
    total = functools.reduce(jnp.add, [r_ref[i, 0:128, :].astype(F32) for i in range(16)])
    column = functools.reduce(
        jnp.add, [column_of(r_ref[i, 128:144, :].astype(F32)) for i in range(16)]
    )
    sums = jnp.concatenate(split3(column) + [jnp.zeros((5, 128), F32)], axis=0)
    for e in range(16):
        pay_ref[e, 0:count, :] = mixed_ref[e]
        pay_ref[e, count : count + 16, :] = jnp.concatenate(
            [total[e * 8 : (e + 1) * 8], sums], axis=0
        ).astype(BF)


def param_expert_kernel(at_ref, r_ref, guess_ref, slot_ref, pay_ref, col_ref):
    count = r_ref.shape[1] - 16
    total = functools.reduce(
        jnp.add, [r_ref[i, count : count + 16, :].astype(F32) for i in range(16)]
    )
    column = column_of(total[8:16])
    col_ref[...] = jnp.broadcast_to(column, (8, 128))
    missed = column - guess_ref[0:1, 0:128]
    lane = lax.broadcasted_iota(jnp.int32, (8, 128), 1)
    row = lax.broadcasted_iota(jnp.int32, (8, 128), 0)
    missed = jnp.sum(
        jnp.where(lane == at_ref[0] * 8 + row, missed, 0.0), axis=1, keepdims=True
    )
    pay_ref[0] = total[0:8] - missed * slot_ref[...]


def token_kernel(
    colown_ref, colother_ref, par_ref, disp_ref, cot_ref, term_ref, in_ref, grad_ref,
    tok_ref, out_ref,
):
    column = jnp.concatenate([colown_ref[0:1, :], colother_ref[0:1, :]], axis=1)
    dispatch = disp_ref[...]
    logit_low = (dispatch * (cot_ref[...] - column) + term_ref[...]).astype(BF)
    token_grad = (nn(dispatch.astype(BF), in_ref[...]) + nn(logit_low, par_ref[...])).astype(BF)
    for f in range(16):
        tok_ref[f] = token_grad[:, f * 128 : (f + 1) * 128]
    out_ref[...] = grad_ref[...]


def param_out_kernel(at_ref, own_ref, other_ref, out_ref):
    first = at_ref[2] == 0
    for f, j in enumerate(chip_order(at_ref)):
        own, other = own_ref[j], other_ref[j]
        out_ref[:, f * 128 : (f + 1) * 128] = jnp.concatenate(
            [jnp.where(first, own, other), jnp.where(first, other, own)], axis=0
        ).astype(BF)


CHIPS = [list(range(0, 32, 2)), list(range(1, 32, 2))]
SIBLING = [(i, i ^ 1) for i in range(32)]


def gather_chips(block):
    for mask in (1, 3, 4, 12):
        pairs = [(i, ((i // 2) ^ mask) * 2 + i % 2) for i in range(32)]
        block = jnp.concatenate([block, lax.ppermute(block, "seq", pairs)], axis=0)
    return block


def swap(array, axis, groups=None):
    return lax.all_to_all(
        array, axis, split_axis=0, concat_axis=0, tiled=True, axis_index_groups=groups
    )


def local(tokens, slot_params, w_in, w_out, out_grad):
    count = tokens.shape[1] // 16
    seq_at = lax.axis_index("seq")
    at = jnp.stack([lax.axis_index("expert"), seq_at // 2, seq_at % 2]).astype(jnp.int32)
    piece = lax.dynamic_slice(
        slot_params, ((seq_at % 2) * 8, (seq_at // 2) * 128), (8, 128)
    )
    by_feature = shape((16, count, 128), BF)
    block = jnp.concatenate(
        [tokens.reshape(by_feature.shape), jnp.broadcast_to(piece[None], (16, 8, 128))], axis=1
    )
    z = swap(block, "expert")
    mine, g = call(
        stage_kernel,
        (shape((1, 128, 128), BF), by_feature),
        z,
        out_grad.reshape(by_feature.shape),
    )
    g = swap(g, "expert")
    params = gather_chips(mine)
    params_other = lax.ppermute(params, "seq", SIBLING)

    half = shape((16, 272, 128), BF)
    slots = shape((count, 256), F32)
    small = shape((16, 24, 128), BF)
    row = shape((8, 128), F32)
    own, other, logits, combine, params = call(
        route_kernel,
        (half, half, slots, slots, shape((256, 2048), BF)),
        at,
        params,
        params_other,
        z,
        g,
    )
    sibling = lax.ppermute(other, "seq", SIBLING)
    pay = call(merge_core_kernel, half, own, sibling)
    pay = call(merge_seq_kernel, small, swap(pay, "seq", CHIPS))
    pay, slot_piece, log_piece = call(
        merge_expert_kernel, (shape((32, 16, 128), BF), row, row), swap(pay, "expert")
    )
    pay, slot_low, grad_low, hidden, pre = call(
        expert_kernel,
        (
            shape((32, 16, 128), BF),
            shape((16, 2048), BF),
            shape((16, 2048), BF),
            shape((16, 128), BF),
            shape((16, 128), BF),
        ),
        swap(pay, "seq"),
        w_in[0],
        w_out[0],
    )
    w_out_grad = tn(hidden, grad_low).astype(BF)
    w_in_grad = tn(slot_low, pre).astype(BF)
    pay = call(out_merge_kernel, small, swap(pay, "seq"), slot_piece, log_piece)
    pay = call(spread_kernel, half, swap(pay, "expert"))
    own = swap(pay, "seq", CHIPS)
    other = lax.ppermute(own, "seq", SIBLING)
    part = shape((16, 144, 128), BF)
    mixed, own, other, guess, dispatch, dispatch_cot, term, ins = call(
        mix_kernel,
        (
            by_feature, part, part, shape((8, 256), F32),
            slots, slots, slots, shape((256, 2048), BF),
        ),
        own,
        other,
        z,
        g,
        logits,
        combine,
    )
    pay = call(param_core_kernel, part, own, lax.ppermute(other, "seq", SIBLING))
    pay = call(
        param_seq_kernel, shape((16, count + 16, 128), BF), swap(pay, "seq", CHIPS), mixed
    )
    pay = swap(pay, "expert")
    mixed = pay[:, 0:count].reshape(tokens.shape)
    param_grad, column = call(
        param_expert_kernel, (shape((1, 8, 128), F32), row), at, pay, guess, slot_piece
    )
    token_grad, param_grad = call(
        token_kernel,
        (by_feature, shape((1, 8, 128), F32)),
        column,
        lax.ppermute(column, "seq", SIBLING),
        params,
        dispatch,
        dispatch_cot,
        term,
        ins,
        param_grad,
    )
    token_grad = swap(token_grad, "expert").reshape(tokens.shape)
    param_grad = gather_chips(param_grad)
    param_grad = call(
        param_out_kernel,
        shape((16, 2048), BF),
        at,
        param_grad,
        lax.ppermute(param_grad, "seq", SIBLING),
    )
    return (mixed, token_grad, param_grad, w_in_grad[None], w_out_grad[None])


def solution(mesh):
    return jax.shard_map(
        local,
        mesh=mesh,
        in_specs=(
            P(None, "seq", "expert"),
            P("expert", None),
            P("expert", None, "seq"),
            P("expert", "seq", None),
            P(None, "seq", "expert"),
        ),
        out_specs=(
            P(None, "seq", "expert"),
            P(None, "seq", "expert"),
            P("expert", None),
            P("expert", None, "seq"),
            P("expert", "seq", None),
        ),
        check_vma=False,
    )
```

```python
import functools

import jax
import jax.numpy as jnp
from jax import lax
from jax.experimental import pallas as pl
from jax.experimental.pallas import tpu as pltpu
from jax.sharding import PartitionSpec as P

BF = jnp.bfloat16
F32 = jnp.float32
INTERPRET = False


def call(body, out_shape, *args):
    vmem, smem = (pl.BlockSpec(memory_space=kind) for kind in (pltpu.VMEM, pltpu.SMEM))
    return pl.pallas_call(
        body,
        out_shape=out_shape,
        in_specs=[smem if arg.dtype == jnp.int32 else vmem for arg in args],
        interpret=INTERPRET,
        compiler_params=pltpu.CompilerParams(vmem_limit_bytes=48 * 1024 * 1024),
    )(*args)


def shape(dims, kind):
    return jax.ShapeDtypeStruct(dims, kind)


def nt(a, b):
    return lax.dot_general(a, b, (((1,), (1,)), ((), ())), preferred_element_type=F32)


def tn(a, b):
    return lax.dot_general(a, b, (((0,), (0,)), ((), ())), preferred_element_type=F32)


def nn(a, b):
    return jnp.dot(a, b, preferred_element_type=F32)


def split3(value):
    high = value.astype(BF).astype(F32)
    rest = value - high
    mid = rest.astype(BF).astype(F32)
    return [high, mid, (rest - mid).astype(BF).astype(F32)]


def lanes(ref, rows=slice(None)):
    return jnp.concatenate([ref[f, rows, :] for f in range(16)], axis=1)


def tokens_of(z_ref):
    count = (z_ref.shape[1] - 8) // 2
    return lanes(z_ref, slice(0, count)), lanes(z_ref, slice(count, 2 * count))


def stage_kernel(at_ref, x_ref, g_ref, slot_ref, pay_ref):
    count = x_ref.shape[1]
    feats = pl.ds(pl.multiple_of(at_ref[1] * 128, 128), 128)
    both = slot_ref[:, feats].astype(F32)
    piece = jnp.where(at_ref[2] == 0, both[0:8], both[8:16]).astype(BF)
    for e in range(16):
        pay_ref[e, 0:count, :] = x_ref[e]
        pay_ref[e, count : 2 * count, :] = g_ref[e]
        pay_ref[e, 2 * count : 2 * count + 8, :] = piece


def route_kernel(pown_ref, pother_ref, z_ref, own_ref, other_ref, logit_ref, comb_ref):
    x, g = tokens_of(z_ref)
    logits = jnp.concatenate([nt(x, lanes(ref)) for ref in (pown_ref, pother_ref)], axis=1)
    logit_ref[...] = logits
    peak = jnp.max(logits, axis=0, keepdims=True)
    raised = jnp.exp(logits - peak)
    total = jnp.sum(raised, axis=0, keepdims=True)
    lifted = jnp.exp(logits - jnp.max(logits, axis=1, keepdims=True))
    combine = lifted / jnp.sum(lifted, axis=1, keepdims=True)
    comb_ref[...] = combine
    stats = jnp.concatenate(
        split3(peak) + split3(total) + [jnp.zeros((10, 256), F32)], axis=0
    ).astype(BF)
    for pay_ref, cols in ((own_ref, slice(0, 128)), (other_ref, slice(128, 256))):
        part_in = tn(raised[:, cols].astype(BF), x).astype(BF)
        part_grad = tn(combine[:, cols].astype(BF), g).astype(BF)
        for f in range(16):
            feats = slice(f * 128, (f + 1) * 128)
            pay_ref[f, 0:128, :] = part_in[:, feats]
            pay_ref[f, 128:256, :] = part_grad[:, feats]
            pay_ref[f, 256:272, :] = stats[:, cols]


def rescale(stats):
    peaks = jnp.concatenate([s[0:1] + s[1:2] + s[2:3] for s in stats], axis=0)
    totals = jnp.concatenate([s[3:4] + s[4:5] + s[5:6] for s in stats], axis=0)
    peak = jnp.max(peaks, axis=0, keepdims=True)
    scale = jnp.exp(peaks - peak)
    total = jnp.sum(scale * totals, axis=0, keepdims=True)
    rows = split3(peak) + split3(total)
    pad = jnp.zeros((122 - len(stats), 128), F32)
    return rows, jnp.concatenate([scale] + rows + [pad], axis=0).T


def merge_core_kernel(own_ref, sib_ref, pay_ref):
    rows, columns = rescale([ref[0, 256:272, :].astype(F32) for ref in (own_ref, sib_ref)])
    stats = jnp.concatenate(rows + [jnp.zeros((10, 128), F32)], axis=0).astype(BF)
    for f in range(16):
        pay_ref[f, 0:128, :] = (
            columns[:, 0:1] * own_ref[f, 0:128, :].astype(F32)
            + columns[:, 1:2] * sib_ref[f, 0:128, :].astype(F32)
        ).astype(BF)
        pay_ref[f, 128:256, :] = (
            own_ref[f, 128:256, :].astype(F32) + sib_ref[f, 128:256, :].astype(F32)
        ).astype(BF)
        pay_ref[f, 256:272, :] = stats


def merge_seq_kernel(r_ref, pay_ref):
    rows, columns = rescale([r_ref[i, 256:272, :].astype(F32) for i in range(16)])
    sum_in = jnp.zeros((128, 128), F32)
    sum_grad = jnp.zeros((128, 128), F32)
    for i in range(16):
        sum_in = sum_in + columns[:, i : i + 1] * r_ref[i, 0:128, :].astype(F32)
        sum_grad = sum_grad + r_ref[i, 128:256, :].astype(F32)
    for e in range(16):
        rows = slice(e * 8, (e + 1) * 8)
        pay_ref[e] = jnp.concatenate(
            [sum_in[rows], sum_grad[rows], columns[rows]], axis=0
        ).astype(BF)


def merge_expert_kernel(r_ref, pay_ref, slot_ref, log_ref):
    blocks = [r_ref[i].astype(F32) for i in range(16)]
    peaks = [b[16:24, 16:17] + b[16:24, 17:18] + b[16:24, 18:19] for b in blocks]
    totals = [b[16:24, 19:20] + b[16:24, 20:21] + b[16:24, 21:22] for b in blocks]
    peak = functools.reduce(jnp.maximum, peaks)
    slot = jnp.zeros((8, 128), F32)
    grad = jnp.zeros((8, 128), F32)
    total = jnp.zeros((8, 1), F32)
    for i in range(16):
        scale = jnp.exp(peaks[i] - peak)
        slot = slot + scale * blocks[i][0:8]
        total = total + scale * totals[i]
        grad = grad + blocks[i][8:16]
    slot = slot / total
    slot_ref[...] = slot
    log_ref[...] = jnp.broadcast_to(peak + jnp.log(total), (8, 128))
    both = jnp.concatenate([slot, grad], axis=0).astype(BF)
    for i in range(32):
        pay_ref[i] = both


def expert_kernel(r_ref, win_ref, wout_ref, pay_ref, slot_ref, grad_ref, hidden_ref, pre_ref):
    blocks = [r_ref[i].astype(F32) for i in range(32)]

    def rows(first):
        return jnp.concatenate(
            [
                jnp.concatenate(
                    [blocks[2 * f][first : first + 8], blocks[2 * f + 1][first : first + 8]],
                    axis=0,
                )
                for f in range(16)
            ],
            axis=1,
        ).astype(BF)

    slot, grad = rows(0), rows(8)
    preact = nn(slot, win_ref[...])
    cdf = 0.5 * (1.0 + lax.erf(preact * 0.7071067811865476))
    density = 0.3989422804014327 * jnp.exp(-0.5 * preact * preact)
    hidden = (preact * cdf).astype(BF)
    hidden_grad = nt(grad, wout_ref[...])
    pre = (hidden_grad * (cdf + preact * density)).astype(BF)
    out_part = nn(hidden, wout_ref[...])
    in_part = nt(pre, win_ref[...])
    for h in range(2):
        for f in range(16):
            rows_, feats = slice(h * 8, h * 8 + 8), slice(f * 128, (f + 1) * 128)
            pay_ref[f * 2 + h] = jnp.concatenate(
                [out_part[rows_, feats], in_part[rows_, feats]], axis=0
            ).astype(BF)
    slot_ref[...] = slot
    grad_ref[...] = grad
    hidden_ref[...] = hidden
    pre_ref[...] = pre


def out_merge_kernel(r_ref, slot_ref, log_ref, pay_ref):
    both = functools.reduce(jnp.add, [r_ref[i].astype(F32) for i in range(32)])
    both = both.astype(BF).astype(F32)
    guess = jnp.sum(both[8:16] * slot_ref[...], axis=1, keepdims=True)
    lane = lax.broadcasted_iota(jnp.int32, (8, 128), 1)
    stats = jnp.zeros((8, 128), F32)
    for at, value in enumerate(split3(log_ref[...][:, 0:1]) + split3(guess)):
        stats = jnp.where(lane == at, value, stats)
    both = jnp.concatenate([both, stats], axis=0).astype(BF)
    for i in range(16):
        pay_ref[i] = both


def spread_kernel(r_ref, pay_ref):
    blocks = [r_ref[i].astype(F32) for i in range(16)]
    out = jnp.concatenate([b[0:8] for b in blocks], axis=0).astype(BF)
    inp = jnp.concatenate([b[8:16] for b in blocks], axis=0).astype(BF)
    stats = jnp.concatenate([b[16:24] for b in blocks], axis=0).T[0:16].astype(BF)
    for i in range(16):
        pay_ref[i, 0:128, :] = out
        pay_ref[i, 128:256, :] = inp
        pay_ref[i, 256:272, :] = stats


def mix_kernel(
    own_ref, other_ref, z_ref, logit_ref, comb_ref,
    mixed_ref, parown_ref, parother_ref, guess_ref, disp_ref, cot_ref, term_ref, in_ref,
):
    x, g = tokens_of(z_ref)
    combine = comb_ref[...]
    combine_low = combine.astype(BF)
    pair = (own_ref, other_ref)
    stats = [ref[0, 256:272, :].astype(F32) for ref in pair]
    logs = jnp.concatenate([s[0:1] + s[1:2] + s[2:3] for s in stats], axis=1)
    sums = [
        functools.reduce(jnp.add, [ref[f, 256:272, :].astype(F32) for f in range(16)])
        for ref in pair
    ]
    guess = jnp.concatenate([s[3:4] + s[4:5] + s[5:6] for s in sums], axis=1)
    outs = jnp.concatenate([lanes(ref, slice(0, 128)) for ref in pair], axis=0)
    ins = jnp.concatenate([lanes(ref, slice(128, 256)) for ref in pair], axis=0)
    dispatch_cot = nt(x, ins)
    dispatch = jnp.exp(logit_ref[...] - logs)
    column = jnp.sum(dispatch.astype(BF).astype(F32) * dispatch_cot, axis=0, keepdims=True)
    combine_cot = nt(g, outs)
    row_sum = jnp.sum(combine_low.astype(F32) * combine_cot, axis=1, keepdims=True)
    term = combine * (combine_cot - row_sum)
    logit_low = (dispatch * (dispatch_cot - guess) + term).astype(BF)
    for ref, half in ((parown_ref, slice(0, 128)), (parother_ref, slice(128, 256))):
        part = tn(logit_low[:, half], x).astype(BF)
        sums = jnp.concatenate(
            split3(column[:, half]) + [jnp.zeros((13, 128), F32)], axis=0
        ).astype(BF)
        for f in range(16):
            ref[f, 0:128, :] = part[:, f * 128 : (f + 1) * 128]
            ref[f, 128:144, :] = sums
    mixed = nn(combine_low, outs).astype(BF)
    for f in range(16):
        mixed_ref[f] = mixed[:, f * 128 : (f + 1) * 128]
    guess_ref[...] = jnp.broadcast_to(guess, (8, 256))
    disp_ref[...] = dispatch
    cot_ref[...] = dispatch_cot
    term_ref[...] = term
    in_ref[...] = ins


def column_of(block):
    return block[0:1] + block[1:2] + block[2:3]


def param_core_kernel(own_ref, sib_ref, pay_ref):
    sums = [ref[0, 128:144, :].astype(F32) for ref in (own_ref, sib_ref)]
    sums = jnp.concatenate(
        split3(column_of(sums[0]) + column_of(sums[1])) + [jnp.zeros((13, 128), F32)], axis=0
    ).astype(BF)
    for f in range(16):
        pay_ref[f, 0:128, :] = (
            own_ref[f, 0:128, :].astype(F32) + sib_ref[f, 0:128, :].astype(F32)
        ).astype(BF)
        pay_ref[f, 128:144, :] = sums


def param_seq_kernel(r_ref, mixed_ref, pay_ref):
    count = mixed_ref.shape[1]
    total = functools.reduce(jnp.add, [r_ref[i, 0:128, :].astype(F32) for i in range(16)])
    column = functools.reduce(
        jnp.add, [column_of(r_ref[i, 128:144, :].astype(F32)) for i in range(16)]
    )
    sums = jnp.concatenate(split3(column) + [jnp.zeros((5, 128), F32)], axis=0)
    for e in range(16):
        pay_ref[e, 0:count, :] = mixed_ref[e]
        pay_ref[e, count : count + 16, :] = jnp.concatenate(
            [total[e * 8 : (e + 1) * 8], sums], axis=0
        ).astype(BF)


def param_expert_kernel(at_ref, r_ref, guess_ref, slot_ref, pay_ref, col_ref):
    count = r_ref.shape[1] - 16
    total = functools.reduce(
        jnp.add, [r_ref[i, count : count + 16, :].astype(F32) for i in range(16)]
    )
    column = column_of(total[8:16])
    col_ref[...] = jnp.broadcast_to(column, (8, 128))
    missed = column - guess_ref[0:1, 0:128]
    lane = lax.broadcasted_iota(jnp.int32, (8, 128), 1)
    row = lax.broadcasted_iota(jnp.int32, (8, 128), 0)
    missed = jnp.sum(
        jnp.where(lane == at_ref[0] * 8 + row, missed, 0.0), axis=1, keepdims=True
    )
    param = (total[0:8] - missed * slot_ref[...]).astype(BF)
    for i in range(16):
        pay_ref[i] = param


def token_kernel(
    colown_ref, colother_ref, pown_ref, pother_ref, disp_ref, cot_ref, term_ref, in_ref, tok_ref
):
    column = jnp.concatenate([colown_ref[0:1, :], colother_ref[0:1, :]], axis=1)
    params = jnp.concatenate([lanes(pown_ref), lanes(pother_ref)], axis=0)
    dispatch = disp_ref[...]
    logit_low = (dispatch * (cot_ref[...] - column) + term_ref[...]).astype(BF)
    token_grad = (nn(dispatch.astype(BF), in_ref[...]) + nn(logit_low, params)).astype(BF)
    for f in range(16):
        tok_ref[f] = token_grad[:, f * 128 : (f + 1) * 128]


def param_out_kernel(at_ref, own_ref, other_ref, out_ref):
    first = at_ref[2] == 0
    for f in range(16):
        own, other = own_ref[f].astype(F32), other_ref[f].astype(F32)
        out_ref[:, f * 128 : (f + 1) * 128] = jnp.concatenate(
            [jnp.where(first, own, other), jnp.where(first, other, own)], axis=0
        ).astype(BF)


CHIPS = [list(range(0, 32, 2)), list(range(1, 32, 2))]
SIBLING = [(i, i ^ 1) for i in range(32)]


def swap(array, axis, groups=None):
    return lax.all_to_all(
        array, axis, split_axis=0, concat_axis=0, tiled=True, axis_index_groups=groups
    )


def local(tokens, slot_params, w_in, w_out, out_grad):
    count = tokens.shape[1] // 16
    seq_at = lax.axis_index("seq")
    at = jnp.stack([lax.axis_index("expert"), seq_at // 2, seq_at % 2]).astype(jnp.int32)
    by_feature = shape((16, count, 128), BF)
    block = call(
        stage_kernel,
        shape((16, 2 * count + 8, 128), BF),
        at,
        tokens.reshape(by_feature.shape),
        out_grad.reshape(by_feature.shape),
        slot_params,
    )
    z = swap(block, "expert")
    mine = z[:, 2 * count :].reshape(128, 128)
    params = swap(jnp.broadcast_to(mine[None], (16, 128, 128)), "seq", CHIPS)
    params_other = lax.ppermute(params, "seq", SIBLING)

    half = shape((16, 272, 128), BF)
    slots = shape((count, 256), F32)
    small = shape((16, 24, 128), BF)
    row = shape((8, 128), F32)
    own, other, logits, combine = call(
        route_kernel, (half, half, slots, slots), params, params_other, z
    )
    sibling = lax.ppermute(other, "seq", SIBLING)
    pay = call(merge_core_kernel, half, own, sibling)
    pay = call(merge_seq_kernel, small, swap(pay, "seq", CHIPS))
    pay, slot_piece, log_piece = call(
        merge_expert_kernel, (shape((32, 16, 128), BF), row, row), swap(pay, "expert")
    )
    pay, slot_low, grad_low, hidden, pre = call(
        expert_kernel,
        (
            shape((32, 16, 128), BF),
            shape((16, 2048), BF),
            shape((16, 2048), BF),
            shape((16, 128), BF),
            shape((16, 128), BF),
        ),
        swap(pay, "seq"),
        w_in[0],
        w_out[0],
    )
    w_out_grad = tn(hidden, grad_low).astype(BF)
    w_in_grad = tn(slot_low, pre).astype(BF)
    pay = call(out_merge_kernel, small, swap(pay, "seq"), slot_piece, log_piece)
    pay = call(spread_kernel, half, swap(pay, "expert"))
    own = swap(pay, "seq", CHIPS)
    other = lax.ppermute(own, "seq", SIBLING)
    part = shape((16, 144, 128), BF)
    mixed, own, other, guess, dispatch, dispatch_cot, term, ins = call(
        mix_kernel,
        (
            by_feature, part, part, shape((8, 256), F32),
            slots, slots, slots, shape((256, 2048), BF),
        ),
        own,
        other,
        z,
        logits,
        combine,
    )
    pay = call(param_core_kernel, part, own, lax.ppermute(other, "seq", SIBLING))
    pay = call(
        param_seq_kernel, shape((16, count + 16, 128), BF), swap(pay, "seq", CHIPS), mixed
    )
    pay = swap(pay, "expert")
    mixed = pay[:, 0:count].reshape(tokens.shape)
    param_grad, column = call(
        param_expert_kernel, (shape((16, 8, 128), BF), row), at, pay, guess, slot_piece
    )
    token_grad = call(
        token_kernel,
        by_feature,
        column,
        lax.ppermute(column, "seq", SIBLING),
        params,
        params_other,
        dispatch,
        dispatch_cot,
        term,
        ins,
    )
    token_grad = swap(token_grad, "expert").reshape(tokens.shape)
    param_grad = swap(param_grad, "seq", CHIPS)
    param_grad = call(
        param_out_kernel,
        shape((16, 2048), BF),
        at,
        param_grad,
        lax.ppermute(param_grad, "seq", SIBLING),
    )
    return (mixed, token_grad, param_grad, w_in_grad[None], w_out_grad[None])


def solution(mesh):
    return jax.shard_map(
        local,
        mesh=mesh,
        in_specs=(
            P(None, "seq", "expert"),
            P("expert", None),
            P("expert", None, "seq"),
            P("expert", "seq", None),
            P(None, "seq", "expert"),
        ),
        out_specs=(
            P(None, "seq", "expert"),
            P(None, "seq", "expert"),
            P("expert", None),
            P("expert", None, "seq"),
            P("expert", "seq", None),
        ),
        check_vma=False,
    )
```

```python
import functools

import jax
import jax.numpy as jnp
from jax import lax
from jax.experimental import pallas as pl
from jax.experimental.pallas import tpu as pltpu
from jax.sharding import PartitionSpec as P

BF = jnp.bfloat16
F32 = jnp.float32
INTERPRET = False


def call(body, out_shape, *args):
    vmem, smem = (pl.BlockSpec(memory_space=kind) for kind in (pltpu.VMEM, pltpu.SMEM))
    return pl.pallas_call(
        body,
        out_shape=out_shape,
        in_specs=[smem if arg.dtype == jnp.int32 else vmem for arg in args],
        interpret=INTERPRET,
        compiler_params=pltpu.CompilerParams(vmem_limit_bytes=48 * 1024 * 1024),
    )(*args)


def shape(dims, kind):
    return jax.ShapeDtypeStruct(dims, kind)


def nt(a, b):
    return lax.dot_general(a, b, (((1,), (1,)), ((), ())), preferred_element_type=F32)


def tn(a, b):
    return lax.dot_general(a, b, (((0,), (0,)), ((), ())), preferred_element_type=F32)


def nn(a, b):
    return jnp.dot(a, b, preferred_element_type=F32)


def split3(value):
    high = value.astype(BF).astype(F32)
    rest = value - high
    mid = rest.astype(BF).astype(F32)
    return [high, mid, (rest - mid).astype(BF).astype(F32)]


def lanes(ref, rows=slice(None)):
    return jnp.concatenate([ref[f, rows, :] for f in range(16)], axis=1)


def stage_kernel(at_ref, x_ref, g_ref, slot_ref, pay_ref):
    count = x_ref.shape[1]
    feats = pl.ds(pl.multiple_of(at_ref[1] * 128, 128), 128)
    both = slot_ref[:, feats].astype(F32)
    piece = jnp.where(at_ref[2] == 0, both[0:8], both[8:16]).astype(BF)
    for e in range(16):
        pay_ref[e, 0:count, :] = x_ref[e]
        pay_ref[e, count : 2 * count, :] = g_ref[e]
        pay_ref[e, 2 * count : 2 * count + 8, :] = piece


def route_kernel(p_ref, z_ref, sib_ref, logit_ref, stat_ref, x_ref, g_ref):
    count = (z_ref.shape[1] - 8) // 2
    for at, ref in enumerate((z_ref, sib_ref)):
        rows = slice(at * count, (at + 1) * count)
        x_ref[rows, :] = lanes(ref, slice(0, count))
        g_ref[rows, :] = lanes(ref, slice(count, 2 * count))
    logits = nt(x_ref[...], lanes(p_ref))
    logit_ref[...] = logits
    peak = jnp.max(logits, axis=1, keepdims=True)
    total = jnp.sum(jnp.exp(logits - peak), axis=1, keepdims=True)
    lane = lax.broadcasted_iota(jnp.int32, logits.shape, 1)
    stat_ref[...] = jnp.where(lane == 0, peak, total)


def swapped(ref):
    count = ref.shape[0] // 2
    return jnp.concatenate([ref[count:, :], ref[:count, :]], axis=0)


def share_kernel(logit_ref, stat_ref, sib_ref, x_ref, g_ref, pay_ref, comb_ref):
    logits = logit_ref[...]
    peak = jnp.max(logits, axis=0, keepdims=True)
    raised = jnp.exp(logits - peak)
    total = jnp.sum(raised, axis=0, keepdims=True)
    mine, other = stat_ref[...], swapped(sib_ref)
    top = jnp.maximum(mine[:, 0:1], other[:, 0:1])
    over = mine[:, 1:2] * jnp.exp(mine[:, 0:1] - top) + other[:, 1:2] * jnp.exp(
        other[:, 0:1] - top
    )
    combine = jnp.exp(logits - top) / over
    comb_ref[...] = combine
    stats = jnp.concatenate(
        split3(peak) + split3(total) + [jnp.zeros((10, 128), F32)], axis=0
    ).astype(BF)
    part_in = tn(raised.astype(BF), x_ref[...]).astype(BF)
    part_grad = tn(combine.astype(BF), g_ref[...]).astype(BF)
    for f in range(16):
        feats = slice(f * 128, (f + 1) * 128)
        pay_ref[f, 0:128, :] = part_in[:, feats]
        pay_ref[f, 128:256, :] = part_grad[:, feats]
        pay_ref[f, 256:272, :] = stats


def rescale(stats):
    peaks = jnp.concatenate([s[0:1] + s[1:2] + s[2:3] for s in stats], axis=0)
    totals = jnp.concatenate([s[3:4] + s[4:5] + s[5:6] for s in stats], axis=0)
    peak = jnp.max(peaks, axis=0, keepdims=True)
    scale = jnp.exp(peaks - peak)
    total = jnp.sum(scale * totals, axis=0, keepdims=True)
    rows = split3(peak) + split3(total)
    pad = jnp.zeros((122 - len(stats), 128), F32)
    return rows, jnp.concatenate([scale] + rows + [pad], axis=0).T


def merge_seq_kernel(r_ref, pay_ref):
    rows, columns = rescale([r_ref[i, 256:272, :].astype(F32) for i in range(16)])
    sum_in = jnp.zeros((128, 128), F32)
    sum_grad = jnp.zeros((128, 128), F32)
    for i in range(16):
        sum_in = sum_in + columns[:, i : i + 1] * r_ref[i, 0:128, :].astype(F32)
        sum_grad = sum_grad + r_ref[i, 128:256, :].astype(F32)
    for e in range(16):
        rows = slice(e * 8, (e + 1) * 8)
        pay_ref[e] = jnp.concatenate(
            [sum_in[rows], sum_grad[rows], columns[rows]], axis=0
        ).astype(BF)


def merge_expert_kernel(r_ref, pay_ref, slot_ref, log_ref):
    blocks = [r_ref[i].astype(F32) for i in range(16)]
    peaks = [b[16:24, 16:17] + b[16:24, 17:18] + b[16:24, 18:19] for b in blocks]
    totals = [b[16:24, 19:20] + b[16:24, 20:21] + b[16:24, 21:22] for b in blocks]
    peak = functools.reduce(jnp.maximum, peaks)
    slot = jnp.zeros((8, 128), F32)
    grad = jnp.zeros((8, 128), F32)
    total = jnp.zeros((8, 1), F32)
    for i in range(16):
        scale = jnp.exp(peaks[i] - peak)
        slot = slot + scale * blocks[i][0:8]
        total = total + scale * totals[i]
        grad = grad + blocks[i][8:16]
    slot = slot / total
    slot_ref[...] = slot
    log_ref[...] = jnp.broadcast_to(peak + jnp.log(total), (8, 128))
    both = jnp.concatenate([slot, grad], axis=0).astype(BF)
    for i in range(32):
        pay_ref[i] = both


def expert_kernel(r_ref, win_ref, wout_ref, pay_ref, slot_ref, grad_ref, hidden_ref, pre_ref):
    blocks = [r_ref[i].astype(F32) for i in range(32)]

    def rows(first):
        return jnp.concatenate(
            [
                jnp.concatenate(
                    [blocks[2 * f][first : first + 8], blocks[2 * f + 1][first : first + 8]],
                    axis=0,
                )
                for f in range(16)
            ],
            axis=1,
        ).astype(BF)

    slot, grad = rows(0), rows(8)
    preact = nn(slot, win_ref[...])
    cdf = 0.5 * (1.0 + lax.erf(preact * 0.7071067811865476))
    density = 0.3989422804014327 * jnp.exp(-0.5 * preact * preact)
    hidden = (preact * cdf).astype(BF)
    hidden_grad = nt(grad, wout_ref[...])
    pre = (hidden_grad * (cdf + preact * density)).astype(BF)
    out_part = nn(hidden, wout_ref[...])
    in_part = nt(pre, win_ref[...])
    for h in range(2):
        for f in range(16):
            rows_, feats = slice(h * 8, h * 8 + 8), slice(f * 128, (f + 1) * 128)
            pay_ref[f * 2 + h] = jnp.concatenate(
                [out_part[rows_, feats], in_part[rows_, feats]], axis=0
            ).astype(BF)
    slot_ref[...] = slot
    grad_ref[...] = grad
    hidden_ref[...] = hidden
    pre_ref[...] = pre


def out_merge_kernel(r_ref, slot_ref, log_ref, pay_ref):
    both = functools.reduce(jnp.add, [r_ref[i].astype(F32) for i in range(32)])
    both = both.astype(BF).astype(F32)
    guess = jnp.sum(both[8:16] * slot_ref[...], axis=1, keepdims=True)
    lane = lax.broadcasted_iota(jnp.int32, (8, 128), 1)
    stats = jnp.zeros((8, 128), F32)
    for at, value in enumerate(split3(log_ref[...][:, 0:1]) + split3(guess)):
        stats = jnp.where(lane == at, value, stats)
    both = jnp.concatenate([both, stats], axis=0).astype(BF)
    for i in range(16):
        pay_ref[i] = both


def spread_kernel(r_ref, pay_ref):
    blocks = [r_ref[i].astype(F32) for i in range(16)]
    out = jnp.concatenate([b[0:8] for b in blocks], axis=0).astype(BF)
    inp = jnp.concatenate([b[8:16] for b in blocks], axis=0).astype(BF)
    stats = jnp.concatenate([b[16:24] for b in blocks], axis=0).T[0:16].astype(BF)
    for i in range(16):
        pay_ref[i, 0:128, :] = out
        pay_ref[i, 128:256, :] = inp
        pay_ref[i, 256:272, :] = stats


def mix_kernel(
    r_ref, x_ref, g_ref, logit_ref, comb_ref,
    mixed_ref, other_ref, row_ref, guess_ref, col_ref, disp_ref, cot_ref, ccot_ref, in_ref,
):
    count = mixed_ref.shape[0]
    combine_low = comb_ref[...].astype(BF)
    stats = [r_ref[f, 256:272, :].astype(F32) for f in range(16)]
    guess = functools.reduce(jnp.add, stats)
    guess = guess[3:4] + guess[4:5] + guess[5:6]
    outs = lanes(r_ref, slice(0, 128))
    ins = lanes(r_ref, slice(128, 256))
    combine_cot = nt(g_ref[...], outs)
    row = jnp.sum(combine_low.astype(F32) * combine_cot, axis=1, keepdims=True)
    row_ref[...] = jnp.broadcast_to(row, combine_cot.shape)
    dispatch_cot = nt(x_ref[...], ins)
    dispatch = jnp.exp(logit_ref[...] - column_of(stats[0]))
    column = jnp.sum(dispatch.astype(BF).astype(F32) * dispatch_cot, axis=0, keepdims=True)
    mixed = nn(combine_low, outs)
    mixed_ref[...] = mixed[:count]
    other_ref[...] = mixed[count:]
    guess_ref[...] = jnp.broadcast_to(guess, (8, 128))
    col_ref[...] = jnp.broadcast_to(column, (8, 128))
    disp_ref[...] = dispatch
    cot_ref[...] = dispatch_cot
    ccot_ref[...] = combine_cot
    in_ref[...] = ins


def logit_kernel(
    row_ref, sib_ref, guess_ref, col_ref, disp_ref, cot_ref, ccot_ref, comb_ref, x_ref,
    term_ref, pay_ref,
):
    row = row_ref[...] + swapped(sib_ref)
    term = comb_ref[...] * (ccot_ref[...] - row)
    term_ref[...] = term
    logit_low = (disp_ref[...] * (cot_ref[...] - guess_ref[0:1, :]) + term).astype(BF)
    part = tn(logit_low, x_ref[...]).astype(BF)
    sums = jnp.concatenate(
        split3(col_ref[0:1, :]) + [jnp.zeros((13, 128), F32)], axis=0
    ).astype(BF)
    for f in range(16):
        pay_ref[f, 0:128, :] = part[:, f * 128 : (f + 1) * 128]
        pay_ref[f, 128:144, :] = sums


def column_of(block):
    return block[0:1] + block[1:2] + block[2:3]


def param_seq_kernel(r_ref, mixed_ref, sib_ref, pay_ref):
    count = mixed_ref.shape[0]
    total = functools.reduce(jnp.add, [r_ref[i, 0:128, :].astype(F32) for i in range(16)])
    column = functools.reduce(
        jnp.add, [column_of(r_ref[i, 128:144, :].astype(F32)) for i in range(16)]
    )
    sums = jnp.concatenate(split3(column) + [jnp.zeros((5, 128), F32)], axis=0)
    for e in range(16):
        feats = slice(e * 128, (e + 1) * 128)
        pay_ref[e, 0:count, :] = (mixed_ref[:, feats] + sib_ref[:, feats]).astype(BF)
        pay_ref[e, count : count + 16, :] = jnp.concatenate(
            [total[e * 8 : (e + 1) * 8], sums], axis=0
        ).astype(BF)


def param_expert_kernel(at_ref, r_ref, guess_ref, slot_ref, pay_ref, col_ref):
    count = r_ref.shape[1] - 16
    total = functools.reduce(
        jnp.add, [r_ref[i, count : count + 16, :].astype(F32) for i in range(16)]
    )
    column = column_of(total[8:16])
    col_ref[...] = jnp.broadcast_to(column, (8, 128))
    missed = column - guess_ref[0:1, :]
    lane = lax.broadcasted_iota(jnp.int32, (8, 128), 1)
    row = lax.broadcasted_iota(jnp.int32, (8, 128), 0)
    missed = jnp.sum(
        jnp.where(lane == at_ref[0] * 8 + row, missed, 0.0), axis=1, keepdims=True
    )
    param = total[0:8] - missed * slot_ref[...]
    for i in range(16):
        pay_ref[i] = param


def token_kernel(
    col_ref, p_ref, disp_ref, cot_ref, term_ref, in_ref, own_ref, other_ref
):
    count = own_ref.shape[0]
    dispatch = disp_ref[...]
    logit_low = (dispatch * (cot_ref[...] - col_ref[0:1, :]) + term_ref[...]).astype(BF)
    token_grad = nn(dispatch.astype(BF), in_ref[...]) + nn(logit_low, lanes(p_ref))
    own_ref[...] = token_grad[:count]
    other_ref[...] = token_grad[count:]


def token_pair_kernel(own_ref, sib_ref, tok_ref):
    for f in range(16):
        feats = slice(f * 128, (f + 1) * 128)
        tok_ref[f] = (own_ref[:, feats] + sib_ref[:, feats]).astype(BF)


def param_out_kernel(at_ref, own_ref, other_ref, out_ref):
    first = at_ref[2] == 0
    for f in range(16):
        own, other = own_ref[f], other_ref[f]
        out_ref[:, f * 128 : (f + 1) * 128] = jnp.concatenate(
            [jnp.where(first, own, other), jnp.where(first, other, own)], axis=0
        ).astype(BF)


CHIPS = [list(range(0, 32, 2)), list(range(1, 32, 2))]
SIBLING = [(i, i ^ 1) for i in range(32)]


def sibling(array):
    return lax.ppermute(array, "seq", SIBLING)


def swap(array, axis, groups=None):
    return lax.all_to_all(
        array, axis, split_axis=0, concat_axis=0, tiled=True, axis_index_groups=groups
    )


def local(tokens, slot_params, w_in, w_out, out_grad):
    count = tokens.shape[1] // 16
    seq_at = lax.axis_index("seq")
    at = jnp.stack([lax.axis_index("expert"), seq_at // 2, seq_at % 2]).astype(jnp.int32)
    by_feature = shape((16, count, 128), BF)
    block = call(
        stage_kernel,
        shape((16, 2 * count + 8, 128), BF),
        at,
        tokens.reshape(by_feature.shape),
        out_grad.reshape(by_feature.shape),
        slot_params,
    )
    z = swap(block, "expert")
    mine = z[:, 2 * count :].reshape(128, 128)
    params = swap(jnp.broadcast_to(mine[None], (16, 128, 128)), "seq", CHIPS)
    z_sibling = sibling(z)

    half = shape((16, 272, 128), BF)
    slots = shape((2 * count, 128), F32)
    wide = shape((2 * count, 2048), BF)
    small = shape((16, 24, 128), BF)
    row = shape((8, 128), F32)
    logits, stats, x, g = call(route_kernel, (slots, slots, wide, wide), params, z, z_sibling)
    pay, combine = call(share_kernel, (half, slots), logits, stats, sibling(stats), x, g)
    pay = call(merge_seq_kernel, small, swap(pay, "seq", CHIPS))
    pay, slot_piece, log_piece = call(
        merge_expert_kernel, (shape((32, 16, 128), BF), row, row), swap(pay, "expert")
    )
    pay, slot_low, grad_low, hidden, pre = call(
        expert_kernel,
        (
            shape((32, 16, 128), BF),
            shape((16, 2048), BF),
            shape((16, 2048), BF),
            shape((16, 128), BF),
            shape((16, 128), BF),
        ),
        swap(pay, "seq"),
        w_in[0],
        w_out[0],
    )
    w_out_grad = tn(hidden, grad_low).astype(BF)
    w_in_grad = tn(slot_low, pre).astype(BF)
    pay = call(out_merge_kernel, small, swap(pay, "seq"), slot_piece, log_piece)
    pay = call(spread_kernel, half, swap(pay, "expert"))
    wide = shape((count, 2048), F32)
    mixed, other, rows, guess, column, dispatch, dispatch_cot, combine_cot, ins = call(
        mix_kernel,
        (wide, wide, slots, row, row, slots, slots, slots, shape((128, 2048), BF)),
        swap(pay, "seq", CHIPS),
        x,
        g,
        logits,
        combine,
    )
    term, pay = call(
        logit_kernel,
        (slots, shape((16, 144, 128), BF)),
        rows,
        sibling(rows),
        guess,
        column,
        dispatch,
        dispatch_cot,
        combine_cot,
        combine,
        x,
    )
    pay = call(
        param_seq_kernel,
        shape((16, count + 16, 128), BF),
        swap(pay, "seq", CHIPS),
        mixed,
        sibling(other),
    )
    pay = swap(pay, "expert")
    mixed = pay[:, 0:count].reshape(tokens.shape)
    param_grad, column = call(
        param_expert_kernel, (shape((16, 8, 128), F32), row), at, pay, guess, slot_piece
    )
    own, other = call(
        token_kernel, (wide, wide), column, params, dispatch, dispatch_cot, term, ins
    )
    token_grad = call(token_pair_kernel, by_feature, own, sibling(other))
    token_grad = swap(token_grad, "expert").reshape(tokens.shape)
    param_grad = swap(param_grad, "seq", CHIPS)
    param_grad = call(
        param_out_kernel,
        shape((16, 2048), BF),
        at,
        param_grad,
        sibling(param_grad),
    )
    return (mixed, token_grad, param_grad, w_in_grad[None], w_out_grad[None])


def solution(mesh):
    return jax.shard_map(
        local,
        mesh=mesh,
        in_specs=(
            P(None, "seq", "expert"),
            P("expert", None),
            P("expert", None, "seq"),
            P("expert", "seq", None),
            P(None, "seq", "expert"),
        ),
        out_specs=(
            P(None, "seq", "expert"),
            P(None, "seq", "expert"),
            P("expert", None),
            P("expert", None, "seq"),
            P("expert", "seq", None),
        ),
        check_vma=False,
    )
```

```python
import functools

import jax
import jax.numpy as jnp
from jax import lax
from jax.experimental import pallas as pl
from jax.experimental.pallas import tpu as pltpu
from jax.sharding import PartitionSpec as P

BF = jnp.bfloat16
F32 = jnp.float32
INTERPRET = False


def call(body, out_shape, *args):
    vmem, smem = (pl.BlockSpec(memory_space=kind) for kind in (pltpu.VMEM, pltpu.SMEM))
    return pl.pallas_call(
        body,
        out_shape=out_shape,
        in_specs=[smem if arg.dtype == jnp.int32 else vmem for arg in args],
        interpret=INTERPRET,
        compiler_params=pltpu.CompilerParams(vmem_limit_bytes=48 * 1024 * 1024),
    )(*args)


def shape(dims, kind):
    return jax.ShapeDtypeStruct(dims, kind)


def nt(a, b):
    return lax.dot_general(a, b, (((1,), (1,)), ((), ())), preferred_element_type=F32)


def tn(a, b):
    return lax.dot_general(a, b, (((0,), (0,)), ((), ())), preferred_element_type=F32)


def nn(a, b):
    return jnp.dot(a, b, preferred_element_type=F32)


def split3(value):
    high = value.astype(BF).astype(F32)
    rest = value - high
    mid = rest.astype(BF).astype(F32)
    return [high, mid, (rest - mid).astype(BF).astype(F32)]


def lanes(ref, rows=slice(None)):
    return jnp.concatenate([ref[f, rows, :] for f in range(16)], axis=1)


def stage_kernel(chip_ref, core_ref, x_ref, g_ref, slot_ref, pay_ref):
    count = x_ref.shape[1]
    feats = pl.ds(pl.multiple_of(chip_ref[0] * 128, 128), 128)
    both = slot_ref[:, feats].astype(F32)
    piece = jnp.where(core_ref[0] == 0, both[0:8], both[8:16]).astype(BF)
    for e in range(16):
        pay_ref[e, 0:count, :] = x_ref[e]
        pay_ref[e, count : 2 * count, :] = g_ref[e]
        pay_ref[e, 2 * count : 2 * count + 8, :] = piece


def split_kernel(z_ref, tok_ref, par_ref):
    count = tok_ref.shape[1]
    piece = jnp.concatenate([z_ref[e].astype(F32)[count:] for e in range(16)], axis=0).astype(BF)
    for i in range(16):
        tok_ref[i] = z_ref[i, 0:count, :]
        par_ref[i] = piece


def route_kernel(p_ref, z_ref, sib_ref, logit_ref, stat_ref, x_ref, g_ref):
    count = z_ref.shape[1] // 2
    for at, ref in enumerate((z_ref, sib_ref)):
        rows = slice(at * count, (at + 1) * count)
        x_ref[rows, :] = lanes(ref, slice(0, count))
        g_ref[rows, :] = lanes(ref, slice(count, 2 * count))
    logits = nt(x_ref[...], lanes(p_ref))
    logit_ref[...] = logits
    peak = jnp.max(logits, axis=1, keepdims=True)
    total = jnp.sum(jnp.exp(logits - peak), axis=1, keepdims=True)
    lane = lax.broadcasted_iota(jnp.int32, logits.shape, 1)
    stat_ref[...] = jnp.where(lane == 0, peak, total)


def swapped(ref):
    count = ref.shape[0] // 2
    return jnp.concatenate([ref[count:, :], ref[:count, :]], axis=0)


def share_kernel(logit_ref, stat_ref, sib_ref, x_ref, g_ref, pay_ref, comb_ref):
    logits = logit_ref[...]
    peak = jnp.max(logits, axis=0, keepdims=True)
    raised = jnp.exp(logits - peak)
    total = jnp.sum(raised, axis=0, keepdims=True)
    mine, other = stat_ref[...], swapped(sib_ref)
    top = jnp.maximum(mine[:, 0:1], other[:, 0:1])
    over = mine[:, 1:2] * jnp.exp(mine[:, 0:1] - top) + other[:, 1:2] * jnp.exp(
        other[:, 0:1] - top
    )
    combine = jnp.exp(logits - top) / over
    comb_ref[...] = combine
    stats = jnp.concatenate(
        split3(peak) + split3(total) + [jnp.zeros((10, 128), F32)], axis=0
    ).astype(BF)
    part_in = tn(raised.astype(BF), x_ref[...]).astype(BF)
    part_grad = tn(combine.astype(BF), g_ref[...]).astype(BF)
    for f in range(16):
        feats = slice(f * 128, (f + 1) * 128)
        pay_ref[f, 0:128, :] = part_in[:, feats]
        pay_ref[f, 128:256, :] = part_grad[:, feats]
        pay_ref[f, 256:272, :] = stats


def rescale(stats):
    peaks = jnp.concatenate([s[0:1] + s[1:2] + s[2:3] for s in stats], axis=0)
    totals = jnp.concatenate([s[3:4] + s[4:5] + s[5:6] for s in stats], axis=0)
    peak = jnp.max(peaks, axis=0, keepdims=True)
    scale = jnp.exp(peaks - peak)
    total = jnp.sum(scale * totals, axis=0, keepdims=True)
    rows = split3(peak) + split3(total)
    pad = jnp.zeros((122 - len(stats), 128), F32)
    return rows, jnp.concatenate([scale] + rows + [pad], axis=0).T


def merge_seq_kernel(r_ref, pay_ref):
    rows, columns = rescale([r_ref[i, 256:272, :].astype(F32) for i in range(16)])
    sum_in = jnp.zeros((128, 128), F32)
    sum_grad = jnp.zeros((128, 128), F32)
    for i in range(16):
        sum_in = sum_in + columns[:, i : i + 1] * r_ref[i, 0:128, :].astype(F32)
        sum_grad = sum_grad + r_ref[i, 128:256, :].astype(F32)
    for e in range(16):
        rows = slice(e * 8, (e + 1) * 8)
        pay_ref[e] = jnp.concatenate(
            [sum_in[rows], sum_grad[rows], columns[rows]], axis=0
        ).astype(BF)


def merge_expert_kernel(r_ref, pay_ref, slot_ref, log_ref):
    blocks = [r_ref[i].astype(F32) for i in range(16)]
    peaks = [b[16:24, 16:17] + b[16:24, 17:18] + b[16:24, 18:19] for b in blocks]
    totals = [b[16:24, 19:20] + b[16:24, 20:21] + b[16:24, 21:22] for b in blocks]
    peak = functools.reduce(jnp.maximum, peaks)
    slot = jnp.zeros((8, 128), F32)
    grad = jnp.zeros((8, 128), F32)
    total = jnp.zeros((8, 1), F32)
    for i in range(16):
        scale = jnp.exp(peaks[i] - peak)
        slot = slot + scale * blocks[i][0:8]
        total = total + scale * totals[i]
        grad = grad + blocks[i][8:16]
    slot = slot / total
    slot_ref[...] = slot
    log_ref[...] = jnp.broadcast_to(peak + jnp.log(total), (8, 128))
    both = jnp.concatenate([slot, grad], axis=0).astype(BF)
    for i in range(32):
        pay_ref[i] = both


def expert_kernel(r_ref, win_ref, wout_ref, pay_ref, slot_ref, grad_ref, hidden_ref, pre_ref):
    blocks = [r_ref[i].astype(F32) for i in range(32)]

    def rows(first):
        return jnp.concatenate(
            [
                jnp.concatenate(
                    [blocks[2 * f][first : first + 8], blocks[2 * f + 1][first : first + 8]],
                    axis=0,
                )
                for f in range(16)
            ],
            axis=1,
        ).astype(BF)

    slot, grad = rows(0), rows(8)
    preact = nn(slot, win_ref[...])
    cdf = 0.5 * (1.0 + lax.erf(preact * 0.7071067811865476))
    density = 0.3989422804014327 * jnp.exp(-0.5 * preact * preact)
    hidden = (preact * cdf).astype(BF)
    hidden_grad = nt(grad, wout_ref[...])
    pre = (hidden_grad * (cdf + preact * density)).astype(BF)
    out_part = nn(hidden, wout_ref[...])
    in_part = nt(pre, win_ref[...])
    for h in range(2):
        for f in range(16):
            rows_, feats = slice(h * 8, h * 8 + 8), slice(f * 128, (f + 1) * 128)
            pay_ref[f * 2 + h] = jnp.concatenate(
                [out_part[rows_, feats], in_part[rows_, feats]], axis=0
            ).astype(BF)
    slot_ref[...] = slot
    grad_ref[...] = grad
    hidden_ref[...] = hidden
    pre_ref[...] = pre


def out_merge_kernel(r_ref, slot_ref, log_ref, pay_ref):
    both = functools.reduce(jnp.add, [r_ref[i].astype(F32) for i in range(32)])
    both = both.astype(BF).astype(F32)
    guess = jnp.sum(both[8:16] * slot_ref[...], axis=1, keepdims=True)
    lane = lax.broadcasted_iota(jnp.int32, (8, 128), 1)
    stats = jnp.zeros((8, 128), F32)
    for at, value in enumerate(split3(log_ref[...][:, 0:1]) + split3(guess)):
        stats = jnp.where(lane == at, value, stats)
    both = jnp.concatenate([both, stats], axis=0).astype(BF)
    for i in range(16):
        pay_ref[i] = both


def spread_kernel(r_ref, pay_ref):
    blocks = [r_ref[i].astype(F32) for i in range(16)]
    out = jnp.concatenate([b[0:8] for b in blocks], axis=0).astype(BF)
    inp = jnp.concatenate([b[8:16] for b in blocks], axis=0).astype(BF)
    stats = jnp.concatenate([b[16:24] for b in blocks], axis=0).T[0:16].astype(BF)
    for i in range(16):
        pay_ref[i, 0:128, :] = out
        pay_ref[i, 128:256, :] = inp
        pay_ref[i, 256:272, :] = stats


def mix_kernel(
    r_ref, x_ref, g_ref, logit_ref, comb_ref,
    mixed_ref, other_ref, row_ref, guess_ref, col_ref, disp_ref, cot_ref, ccot_ref, in_ref,
):
    count = mixed_ref.shape[0]
    combine_low = comb_ref[...].astype(BF)
    stats = [r_ref[f, 256:272, :].astype(F32) for f in range(16)]
    guess = functools.reduce(jnp.add, stats)
    guess = guess[3:4] + guess[4:5] + guess[5:6]
    outs = lanes(r_ref, slice(0, 128))
    ins = lanes(r_ref, slice(128, 256))
    combine_cot = nt(g_ref[...], outs)
    row = jnp.sum(combine_low.astype(F32) * combine_cot, axis=1, keepdims=True)
    row_ref[...] = jnp.broadcast_to(row, combine_cot.shape)
    dispatch_cot = nt(x_ref[...], ins)
    dispatch = jnp.exp(logit_ref[...] - column_of(stats[0]))
    column = jnp.sum(dispatch.astype(BF).astype(F32) * dispatch_cot, axis=0, keepdims=True)
    mixed = nn(combine_low, outs)
    mixed_ref[...] = mixed[:count]
    other_ref[...] = mixed[count:]
    guess_ref[...] = jnp.broadcast_to(guess, (8, 128))
    col_ref[...] = jnp.broadcast_to(column, (8, 128))
    disp_ref[...] = dispatch
    cot_ref[...] = dispatch_cot
    ccot_ref[...] = combine_cot
    in_ref[...] = ins


def logit_kernel(
    row_ref, sib_ref, guess_ref, col_ref, disp_ref, cot_ref, ccot_ref, comb_ref, x_ref,
    term_ref, pay_ref,
):
    row = row_ref[...] + swapped(sib_ref)
    term = comb_ref[...] * (ccot_ref[...] - row)
    term_ref[...] = term
    logit_low = (disp_ref[...] * (cot_ref[...] - guess_ref[0:1, :]) + term).astype(BF)
    part = tn(logit_low, x_ref[...]).astype(BF)
    sums = jnp.concatenate(
        split3(col_ref[0:1, :]) + [jnp.zeros((13, 128), F32)], axis=0
    ).astype(BF)
    for f in range(16):
        pay_ref[f, 0:128, :] = part[:, f * 128 : (f + 1) * 128]
        pay_ref[f, 128:144, :] = sums


def column_of(block):
    return block[0:1] + block[1:2] + block[2:3]


def param_seq_kernel(r_ref, mixed_ref, sib_ref, pay_ref):
    count = mixed_ref.shape[0]
    total = functools.reduce(jnp.add, [r_ref[i, 0:128, :].astype(F32) for i in range(16)])
    column = functools.reduce(
        jnp.add, [column_of(r_ref[i, 128:144, :].astype(F32)) for i in range(16)]
    )
    sums = jnp.concatenate(split3(column) + [jnp.zeros((5, 128), F32)], axis=0)
    for e in range(16):
        feats = slice(e * 128, (e + 1) * 128)
        pay_ref[e, 0:count, :] = (mixed_ref[:, feats] + sib_ref[:, feats]).astype(BF)
        pay_ref[e, count : count + 16, :] = jnp.concatenate(
            [total[e * 8 : (e + 1) * 8], sums], axis=0
        ).astype(BF)


def param_expert_kernel(at_ref, r_ref, guess_ref, slot_ref, pay_ref, col_ref):
    count = r_ref.shape[1] - 16
    total = functools.reduce(
        jnp.add, [r_ref[i, count : count + 16, :].astype(F32) for i in range(16)]
    )
    column = column_of(total[8:16])
    col_ref[...] = jnp.broadcast_to(column, (8, 128))
    missed = column - guess_ref[0:1, :]
    lane = lax.broadcasted_iota(jnp.int32, (8, 128), 1)
    row = lax.broadcasted_iota(jnp.int32, (8, 128), 0)
    missed = jnp.sum(
        jnp.where(lane == at_ref[0] * 8 + row, missed, 0.0), axis=1, keepdims=True
    )
    param = total[0:8] - missed * slot_ref[...]
    for i in range(16):
        pay_ref[i] = param


def token_kernel(
    col_ref, p_ref, disp_ref, cot_ref, term_ref, in_ref, own_ref, other_ref
):
    count = own_ref.shape[0]
    dispatch = disp_ref[...]
    logit_low = (dispatch * (cot_ref[...] - col_ref[0:1, :]) + term_ref[...]).astype(BF)
    token_grad = nn(dispatch.astype(BF), in_ref[...]) + nn(logit_low, lanes(p_ref))
    own_ref[...] = token_grad[:count]
    other_ref[...] = token_grad[count:]


def token_pair_kernel(own_ref, sib_ref, tok_ref):
    for f in range(16):
        feats = slice(f * 128, (f + 1) * 128)
        tok_ref[f] = (own_ref[:, feats] + sib_ref[:, feats]).astype(BF)


def param_out_kernel(core_ref, own_ref, other_ref, out_ref):
    first = core_ref[0] == 0
    for f in range(16):
        own, other = own_ref[f], other_ref[f]
        out_ref[:, f * 128 : (f + 1) * 128] = jnp.concatenate(
            [jnp.where(first, own, other), jnp.where(first, other, own)], axis=0
        ).astype(BF)


CHIPS = [list(range(0, 32, 2)), list(range(1, 32, 2))]
SIBLING = [(i, i ^ 1) for i in range(32)]


def sibling(array):
    return lax.ppermute(array, "seq", SIBLING)


def swap(array, axis, groups=None):
    return lax.all_to_all(
        array, axis, split_axis=0, concat_axis=0, tiled=True, axis_index_groups=groups
    )


def local(tokens, slot_params, w_in, w_out, out_grad):
    count = tokens.shape[1] // 16
    seq_at = lax.axis_index("seq")
    expert, chip, core = (
        value.astype(jnp.int32).reshape(1)
        for value in (lax.axis_index("expert"), seq_at // 2, seq_at % 2)
    )
    by_feature = shape((16, count, 128), BF)
    block = call(
        stage_kernel,
        shape((16, 2 * count + 8, 128), BF),
        chip,
        core,
        tokens.reshape(by_feature.shape),
        out_grad.reshape(by_feature.shape),
        slot_params,
    )
    z = swap(block, "expert")
    z, params = call(
        split_kernel, (shape((16, 2 * count, 128), BF), shape((16, 128, 128), BF)), z
    )
    params = swap(params, "seq", CHIPS)
    z_sibling = sibling(z)

    half = shape((16, 272, 128), BF)
    slots = shape((2 * count, 128), F32)
    wide = shape((2 * count, 2048), BF)
    small = shape((16, 24, 128), BF)
    row = shape((8, 128), F32)
    logits, stats, x, g = call(route_kernel, (slots, slots, wide, wide), params, z, z_sibling)
    pay, combine = call(share_kernel, (half, slots), logits, stats, sibling(stats), x, g)
    pay = call(merge_seq_kernel, small, swap(pay, "seq", CHIPS))
    pay, slot_piece, log_piece = call(
        merge_expert_kernel, (shape((32, 16, 128), BF), row, row), swap(pay, "expert")
    )
    pay, slot_low, grad_low, hidden, pre = call(
        expert_kernel,
        (
            shape((32, 16, 128), BF),
            shape((16, 2048), BF),
            shape((16, 2048), BF),
            shape((16, 128), BF),
            shape((16, 128), BF),
        ),
        swap(pay, "seq"),
        w_in[0],
        w_out[0],
    )
    w_out_grad = tn(hidden, grad_low).astype(BF)
    w_in_grad = tn(slot_low, pre).astype(BF)
    pay = call(out_merge_kernel, small, swap(pay, "seq"), slot_piece, log_piece)
    pay = call(spread_kernel, half, swap(pay, "expert"))
    wide = shape((count, 2048), F32)
    mixed, other, rows, guess, column, dispatch, dispatch_cot, combine_cot, ins = call(
        mix_kernel,
        (wide, wide, slots, row, row, slots, slots, slots, shape((128, 2048), BF)),
        swap(pay, "seq", CHIPS),
        x,
        g,
        logits,
        combine,
    )
    term, pay = call(
        logit_kernel,
        (slots, shape((16, 144, 128), BF)),
        rows,
        sibling(rows),
        guess,
        column,
        dispatch,
        dispatch_cot,
        combine_cot,
        combine,
        x,
    )
    pay = call(
        param_seq_kernel,
        shape((16, count + 16, 128), BF),
        swap(pay, "seq", CHIPS),
        mixed,
        sibling(other),
    )
    pay = swap(pay, "expert")
    mixed = pay[:, 0:count].reshape(tokens.shape)
    param_grad, column = call(
        param_expert_kernel, (shape((16, 8, 128), F32), row), expert, pay, guess, slot_piece
    )
    own, other = call(
        token_kernel, (wide, wide), column, params, dispatch, dispatch_cot, term, ins
    )
    token_grad = call(token_pair_kernel, by_feature, own, sibling(other))
    token_grad = swap(token_grad, "expert").reshape(tokens.shape)
    param_grad = swap(param_grad, "seq", CHIPS)
    param_grad = call(
        param_out_kernel,
        shape((16, 2048), BF),
        core,
        param_grad,
        sibling(param_grad),
    )
    return (mixed, token_grad, param_grad, w_in_grad[None], w_out_grad[None])


def solution(mesh):
    return jax.shard_map(
        local,
        mesh=mesh,
        in_specs=(
            P(None, "seq", "expert"),
            P("expert", None),
            P("expert", None, "seq"),
            P("expert", "seq", None),
            P(None, "seq", "expert"),
        ),
        out_specs=(
            P(None, "seq", "expert"),
            P(None, "seq", "expert"),
            P("expert", None),
            P("expert", None, "seq"),
            P("expert", "seq", None),
        ),
        check_vma=False,
    )
```
